256 devices in a mesh: dp: 32 (over y_lo, z, core), cores: 8 (over y_hi, x).
Axes of the slice: x: 4, y: 4 (y_hi: 2, y_lo: 2; y = y_hi * 2 + y_lo), z: 8, core: 2. Of those that a mesh axis runs over, the one named last changes fastest.
Arguments:
- tokens: bfloat16 [8192, 6144], P('dp', 'cores'), may hold values from -6 to 6
- router_weight: bfloat16 [256, 6144], P(None, 'cores'), may hold values from -0.078125 to 0.078125
- expert_factor: bfloat16 [256, 64], P(None, 'cores'), may hold values from -0.375 to 0.375
- input_factor: bfloat16 [512, 6144], P(None, 'cores'), may hold values from -0.078125 to 0.078125
- core_tensor: bfloat16 [512, 64, 512], P('dp', 'cores'), may hold values from -0.03125 to 0.03125
- output_factor: bfloat16 [512, 6144], P(None, 'cores'), may hold values from -0.25 to 0.25
- out_grad: bfloat16 [8192, 6144], P('dp', 'cores'), may hold values from -6 to 6
Outputs:
- mixed: bfloat16 [8192, 6144], P('dp', 'cores')
- token_grad: bfloat16 [8192, 6144], P('dp', 'cores')
- core_grad: float32 [512, 64, 512], P('dp', 'cores')
- input_grad: float32 [512, 6144], P('dp', 'cores')
- router_grad: float32 [256, 6144], P('dp', 'cores')
- output_grad: float32 [512, 6144], P('dp', 'cores')
- expert_grad: float32 [256, 64], P('dp', 'cores')
The draws below stay inside these ranges and needn't reach their ends.
All inputs are finite; a program needn't handle non-finite values.
Results may differ from the reference program's by a relative error of at most 0.0066.
Values may be sent and summed in bfloat16 or wider, within the bound.
A program may use at most 64 MiB of HBM per device.

```python
import jax
import jax.numpy as jnp
from jax import lax

D = 6144
E = 256
RE = 64
RI = 512
RO = 512
TOK = 256
TOKENS = 8192
N_DP = 32


def block_scale(stream_key, extent, shards, smallest, high):
    def one(dim, blocks):
        draws = jax.random.uniform(jax.random.fold_in(jax.random.fold_in(stream_key, 6), dim), (blocks,), jnp.float32, smallest / len(shards), high / len(shards))
        return jnp.repeat(jnp.exp(draws), extent[dim] // blocks).reshape((-1,) + (1,) * (len(extent) - dim - 1))

    level = one(*shards[0])
    for cut in shards[1:]:
        level = level * one(*cut)
    return level


def centred(stream_key, shape, scale, bound, pieces=(), held_as=jnp.bfloat16):
    drawn = scale * jax.random.normal(stream_key, shape, jnp.float32)
    if pieces:
        drawn = drawn * block_scale(stream_key, shape, pieces, -0.22, 0.18)
    return jnp.clip(drawn, -bound, bound).astype(held_as)


def setup_inputs(seed: int = 0) -> dict:
    key_of = jax.random.split(jax.random.key(seed), 8)
    tokens = centred(key_of[0], (TOKENS, D), 1.0, 6.0, ((0, 32), (1, 8)))
    router_weight = centred(key_of[1], (E, D), D ** -0.5, 0.078125, ((1, 8),))
    expert_factor = centred(key_of[2], (E, RE), E ** -0.5, 0.375, ((1, 8),))
    input_factor = centred(key_of[3], (RI, D), D ** -0.5, 0.078125, ((1, 8),))
    core_tensor = centred(key_of[4], (RI, RE, RO), (RI * RE) ** -0.5, 0.03125, ((0, 32), (1, 8)))
    output_factor = centred(key_of[5], (RO, D), RO ** -0.5, 0.25, ((1, 8),))
    out_grad = centred(key_of[6], (TOKENS, D), 1.0, 6.0, ((0, 32), (1, 8)))
    return {"tokens": tokens, "router_weight": router_weight, "expert_factor": expert_factor, "input_factor": input_factor, "core_tensor": core_tensor, "output_factor": output_factor, "out_grad": out_grad}


def reference(tokens, router_weight, expert_factor, input_factor, core_tensor, output_factor, out_grad):
    highest = lax.Precision.HIGHEST
    logits = jnp.dot(tokens, router_weight.T, preferred_element_type=jnp.float32)
    gate_values = jax.nn.sigmoid(logits)
    gate_low = gate_values.astype(jnp.bfloat16)
    mixing = jnp.dot(gate_low, expert_factor, preferred_element_type=jnp.float32)
    projected = jnp.dot(tokens, input_factor.T, preferred_element_type=jnp.float32).astype(jnp.bfloat16)
    latent_grad = jnp.dot(out_grad, output_factor.T, preferred_element_type=jnp.float32).astype(jnp.bfloat16)
    core_wide = core_tensor.astype(jnp.float32)

    def per_block(running, inputs):
        proj_block, mix_block, grad_block = inputs
        proj_wide = proj_block.astype(jnp.float32)
        grad_wide = grad_block.astype(jnp.float32)
        expanded = jnp.einsum("ti,ieo->teo", proj_wide, core_wide, precision=highest)
        latent_block = jnp.einsum("te,teo->to", mix_block, expanded, precision=highest).astype(jnp.bfloat16)
        spread = jnp.einsum("to,ieo->tei", grad_wide, core_wide, precision=highest)
        mixing_block = jnp.einsum("ti,tei->te", proj_wide, spread, precision=highest)
        projgrad_block = jnp.einsum("te,tei->ti", mix_block, spread, precision=highest).astype(jnp.bfloat16)
        outer_low = lax.optimization_barrier((mix_block[:, :, None] * grad_wide[:, None, :]).astype(jnp.bfloat16))
        outer = outer_low.astype(jnp.float32)
        running = running + jnp.einsum("ti,teo->ieo", proj_wide, outer, precision=highest)
        return running, (latent_block, mixing_block, projgrad_block)

    inputs = (projected.reshape(N_DP, TOK, RI), mixing.reshape(N_DP, TOK, RE), latent_grad.reshape(N_DP, TOK, RO))
    initial = jnp.zeros((RI, RE, RO), jnp.float32)
    core_sum, outputs = lax.scan(per_block, initial, inputs)
    latent = outputs[0].reshape(TOKENS, RO)
    mixing_grad = outputs[1].reshape(TOKENS, RE)
    projected_grad = outputs[2].reshape(TOKENS, RI)

    mixed = jnp.dot(latent, output_factor, preferred_element_type=jnp.float32).astype(jnp.bfloat16)
    output_grad = jnp.dot(latent.T, out_grad, preferred_element_type=jnp.float32) / TOK
    core_grad = core_sum / TOK
    mixing_low = mixing_grad.astype(jnp.bfloat16)
    gate_grad = jnp.dot(mixing_low, expert_factor.T, preferred_element_type=jnp.float32)
    expert_grad = jnp.dot(gate_low.T, mixing_low, preferred_element_type=jnp.float32) / TOK
    logit_grad = (gate_grad * gate_values * (1.0 - gate_values)).astype(jnp.bfloat16)
    token_sum = jnp.dot(projected_grad, input_factor, preferred_element_type=jnp.float32) + jnp.dot(logit_grad, router_weight, preferred_element_type=jnp.float32)
    token_grad = token_sum.astype(jnp.bfloat16)
    input_grad = jnp.dot(projected_grad.T, tokens, preferred_element_type=jnp.float32) / TOK
    router_grad = jnp.dot(logit_grad.T, tokens, preferred_element_type=jnp.float32) / TOK
    return (mixed, token_grad, core_grad, input_grad, router_grad, output_grad, expert_grad)
```

```python
import functools

import jax
import jax.numpy as jnp
from jax import lax
from jax.experimental import pallas as pl
from jax.experimental.pallas import tpu as pltpu
from jax.sharding import PartitionSpec as P

MESH = pl.DeviceIdType.MESH
F32 = jnp.float32
BF16 = jnp.bfloat16


def dot_nn(a, b):
    return lax.dot_general(a, b, (((1,), (0,)), ((), ())), preferred_element_type=F32)


def dot_nt(a, b):
    return lax.dot_general(a, b, (((1,), (1,)), ((), ())), preferred_element_type=F32)


def dot_tn(a, b):
    return lax.dot_general(a, b, (((0,), (0,)), ((), ())), preferred_element_type=F32)


def ring_hops(n_z):
    up = n_z // 2
    down = n_z - 1 - up
    return ((up, down), (down, up))


class Ids:
    def __init__(self, n_z, n_cores, n_e):
        self.count = 0
        steps = n_z // 2
        self.gather_y = self.take(1)
        self.gather_z = self.take(4 * steps)
        self.gather_sib = self.take(2 * n_z)
        self.factor = self.take(n_cores - 1)
        self.sum_in = self.take(n_cores - 1)
        self.share_in = self.take(n_cores - 1)
        self.sum_mid = self.take(n_cores - 1)
        self.share_mid = self.take(n_cores - 1)
        self.core_sib = self.take(n_e)
        self.core_z = self.take(4 * steps)
        self.core_y = self.take(1)
        self.fac_sib = self.take(1)
        self.fac_z = self.take(4 * steps)
        self.fac_y = self.take(1)

    def take(self, n):
        first = self.count
        self.count += n
        return first


def kernel(
    n_z, n_cores,
    tok_hbm, rw_hbm, ef_hbm, inf_hbm, core_hbm, outf_hbm, og_hbm,
    mixed_ref, tgrad_ref, cgrad_ref, igrad_ref, rgrad_ref, ograd_ref, egrad_ref,
    tok, rw, ef, inf, outf, og,
    whole, ef_all, part_in, got_in, held_in, gates, part_mid, got_mid, held_mid,
    mix_b, outer, lat_acc, pg_acc, mg_acc,
    core_b, core_s, core_r, core_yr,
    fac_b, fac_s, fac_r, fac_yr,
    in_sem, ss, rs,
):
    rows, width = tok.shape
    n_g = rw.shape[0]
    n_i = inf.shape[0]
    n_o = outf.shape[0]
    n_e = ef.shape[0]
    block = rows // n_cores
    i_rows = whole.shape[4]
    n_dp = 4 * n_z
    inv_rows = 1.0 / rows
    ids = Ids(n_z, n_cores, n_e)
    steps = n_z // 2
    hops = ring_hops(n_z)

    dp = lax.axis_index("dp")
    c = lax.axis_index("cores")
    core = lax.rem(dp, 2)
    z = lax.rem(dp // 2, n_z)
    y = dp // (2 * n_z)

    def at(yy, zz, kk):
        return ((yy * n_z + zz) * 2 + kk, c)

    def zmod(offset):
        return lax.rem(z + offset + 2 * n_z, n_z)

    sib = at(y, z, 1 - core)
    ynb = at(1 - y, z, core)
    znb = (at(y, zmod(1), core), at(y, zmod(-1), core))
    n_x = n_cores // 2
    y_hi = c // n_x
    x = lax.rem(c, n_x)
    peers = []
    for dy in range(2):
        for dx in range(n_x):
            if dy or dx:
                other = lax.rem(y_hi + dy, 2) * n_x + lax.rem(x + dx, n_x)
                peers.append((dp, other))

    sent = []

    def send(i, src, dst, dev):
        d = pltpu.make_async_remote_copy(
            src, dst, ss.at[i], rs.at[i], device_id=dev, device_id_type=MESH
        )
        d.start()
        sent.append(d)

    def arrive(i, ref):
        pltpu.make_async_remote_copy(
            ref, ref, ss.at[i], rs.at[i], device_id=sib, device_id_type=MESH
        ).wait_recv()

    loads = [
        pltpu.make_async_copy(src, dst, in_sem.at[n])
        for n, (src, dst) in enumerate(
            (
                (core_hbm, whole.at[y, z, core]),
                (tok_hbm, tok),
                (inf_hbm, inf),
                (og_hbm, og),
                (outf_hbm, outf),
                (rw_hbm, rw),
                (ef_hbm, ef),
            )
        )
    ]
    for load in loads:
        load.start()

    barrier = pltpu.get_barrier_semaphore()
    greet = [sib, ynb, znb[0], znb[1]] + peers
    for dev in greet:
        pl.semaphore_signal(barrier, inc=1, device_id=dev, device_id_type=MESH)
    pl.semaphore_wait(barrier, len(greet))

    lane_y = (y, 1 - y)

    def ag_id(lane, way, s):
        return ids.gather_z + (lane * 2 + way) * steps + s - 1

    def ag_ref(lane, zz):
        return whole.at[lane_y[lane], zz, core]

    def ag_sib(lane, offset):
        ref = ag_ref(lane, zmod(offset))
        send(ids.gather_sib + lane * n_z + offset % n_z, ref, ref, sib)

    def ag_open(lane):
        ref = ag_ref(lane, z)
        for way in range(2):
            if hops[lane][way] >= 1:
                send(ag_id(lane, way, 1), ref, ref, znb[way])
        ag_sib(lane, 0)

    def ag_step(s, lane):
        for way in range(2):
            if s <= hops[lane][way]:
                offset = -s if way == 0 else s
                ref = ag_ref(lane, zmod(offset))
                arrive(ag_id(lane, way, s), ref)
                if s + 1 <= hops[lane][way]:
                    send(ag_id(lane, way, s + 1), ref, ref, znb[way])
                ag_sib(lane, offset)

    def ag_close():
        for lane in range(2):
            for offset in range(n_z):
                ref = whole.at[lane_y[lane], zmod(offset), 1 - core]
                arrive(ids.gather_sib + lane * n_z + offset, ref)

    loads[0].wait()
    send(ids.gather_y, ag_ref(0, z), ag_ref(0, z), ynb)
    ag_open(0)

    loads[6].wait()
    ef_all[c] = ef[...].astype(F32)
    for k, dev in enumerate(peers):
        send(ids.factor + k, ef_all.at[c], ef_all.at[c], dev)
    loads[1].wait()
    loads[2].wait()
    part_in[:, :, n_g : n_g + n_i] = (
        dot_nt(tok[...], inf[...]).reshape(n_cores, block, n_i)
    )
    loads[3].wait()
    loads[4].wait()
    part_in[:, :, n_g + n_i :] = (
        dot_nt(og[...], outf[...]).reshape(n_cores, block, n_o)
    )
    loads[5].wait()
    part_in[:, :, :n_g] = dot_nt(tok[...], rw[...]).reshape(n_cores, block, n_g)
    for k, dev in enumerate(peers):
        send(ids.sum_in + k, part_in.at[dev[1]], got_in.at[k], dev)

    arrive(ids.gather_y, ag_ref(1, z))
    ag_open(1)
    ag_step(1, 0)

    for k in range(n_cores - 1):
        arrive(ids.sum_in + k, got_in.at[k])
    total = part_in[c]
    for k in range(n_cores - 1):
        total = total + got_in[k]
    gate = jax.nn.sigmoid(total[:, :n_g])
    gates[...] = gate
    held_in[c, :, :n_g] = gate.astype(BF16)
    held_in[c, :, n_g:] = total[:, n_g:].astype(BF16)
    for k, dev in enumerate(peers):
        send(ids.share_in + k, held_in.at[c], held_in.at[c], dev)

    ag_step(1, 1)
    ag_step(2, 0)

    for k in range(n_cores - 1):
        ref = held_in.at[peers_from(y_hi, x, n_x)[k]]
        arrive(ids.share_in + k, ref)

    gate_low = held_in[:, :, :n_g].reshape(rows, n_g)
    proj = held_in[:, :, n_g : n_g + n_i].reshape(rows, n_i)
    lgrad = held_in[:, :, n_g + n_i :].reshape(rows, n_o)
    mixing = dot_nt(gate_low, ef[...])
    for e in range(n_e):
        mix_b[e] = jnp.broadcast_to(mixing[:, e : e + 1], (rows, 128))

    def wide(v, n):
        return jnp.concatenate([v] * (n // 128), axis=1)

    proj_t = proj.T
    lgrad_wide = lgrad.astype(F32)

    def core_terms(e, _):
        o = (wide(mix_b[e], n_o) * lgrad_wide).astype(BF16)
        outer[e] = o
        term = dot_nn(proj_t, o) * inv_rows
        core_b[:, :, :, e] = term.astype(BF16).reshape(2, n_z, 2, i_rows, n_o)
        pltpu.make_async_remote_copy(
            core_b.at[:, :, 1 - core, e],
            core_s.at[:, :, e],
            ss.at[ids.core_sib + e],
            rs.at[ids.core_sib + e],
            device_id=sib,
            device_id_type=MESH,
        ).start()
        return 0

    lax.fori_loop(0, n_e, core_terms, 0)

    ag_step(2, 1)
    for s in range(3, steps + 1):
        ag_step(s, 0)
        ag_step(s, 1)

    def rs_step(s, src, sib_got, got, first):
        for lane in range(2):
            for way in range(2):
                k = hops[lane][way]
                if s <= k:
                    far = k - s + 1
                    d = zmod(far if way == 0 else -far)
                    val = src[lane_y[lane], d, core].astype(F32) + sib_got[
                        lane_y[lane], d
                    ].astype(F32)
                    if s > 1:
                        arrive(first + (lane * 2 + way) * steps + s - 2, got.at[lane, way, s - 2])
                        val = val + got[lane, way, s - 2].astype(F32)
                    src[lane_y[lane], d, core] = val.astype(BF16)
                    send(
                        first + (lane * 2 + way) * steps + s - 1,
                        src.at[lane_y[lane], d, core],
                        got.at[lane, way, s - 1],
                        znb[way],
                    )

    def rs_lane(lane, src, sib_got, got, first):
        val = src[lane_y[lane], z, core].astype(F32) + sib_got[lane_y[lane], z].astype(F32)
        for way in range(2):
            k = hops[lane][way]
            if k:
                arrive(first + (lane * 2 + way) * steps + k - 1, got.at[lane, way, k - 1])
                val = val + got[lane, way, k - 1].astype(F32)
        return val

    def rs_turn(src, sib_got, got, yr, first, y_id):
        val = rs_lane(1, src, sib_got, got, first)
        src[1 - y, z, core] = val.astype(BF16)
        send(y_id, src.at[1 - y, z, core], yr, ynb)

    def rs_end(src, sib_got, got, yr, first, y_id):
        val = rs_lane(0, src, sib_got, got, first)
        arrive(y_id, yr)
        return val + yr[...].astype(F32)

    core_args = (core_b, core_s, core_r)
    fac_args = (fac_b, fac_s, fac_r)

    for e in range(n_e):
        arrive(ids.core_sib + e, core_s.at[:, :, e])
    rs_step(1, *core_args, ids.core_z)

    ag_close()

    lat_acc[...] = jnp.zeros_like(lat_acc)
    pg_acc[...] = jnp.zeros_like(pg_acc)
    mg_acc[...] = jnp.zeros_like(mg_acc)
    lane_no = lax.broadcasted_iota(jnp.int32, (rows, 128), 1)

    def middle(e, _):
        core_e = whole[:, :, :, e].reshape(n_i, n_o)
        expanded = dot_nn(proj, core_e)
        lat_acc[...] += wide(mix_b[e], n_o) * expanded
        col = jnp.sum(lgrad_wide * expanded, axis=1, keepdims=True)
        mg_acc[...] += jnp.where(lane_no == c * n_e + e, col, 0.0)
        pg_acc[...] += dot_nt(outer[e], core_e)
        return 0

    lax.fori_loop(0, n_e, middle, 0)

    part_mid[:, :, :n_o] = lat_acc[...].astype(BF16).reshape(n_cores, block, n_o)
    part_mid[:, :, n_o : n_o + n_i] = pg_acc[...].astype(BF16).reshape(n_cores, block, n_i)
    mix_low = mg_acc[...].astype(BF16)
    part_mid[:, :, n_o + n_i :] = mix_low.reshape(n_cores, block, 128)
    for k, dev in enumerate(peers):
        send(ids.sum_mid + k, part_mid.at[dev[1]], got_mid.at[k], dev)

    expert_full = lax.dot_general(
        gate_low, mix_low, (((0,), (0,)), ((), ())), preferred_element_type=F32
    ) * inv_rows
    pick = (
        lax.broadcasted_iota(jnp.int32, (128, 128), 0)
        == lax.broadcasted_iota(jnp.int32, (128, 128), 1) + c * n_e
    ).astype(BF16)
    expert_term = dot_nn(expert_full.astype(BF16), pick)

    rs_step(2, *core_args, ids.core_z)

    for k in range(n_cores - 1):
        arrive(ids.factor + k, ef_all.at[peers_from(y_hi, x, n_x)[k]])
    for k in range(n_cores - 1):
        arrive(ids.sum_mid + k, got_mid.at[k])
    total = part_mid[c].astype(F32)
    for k in range(n_cores - 1):
        total = total + got_mid[k].astype(F32)
    mix_block = total[:, n_o + n_i : n_o + n_i + n_cores * n_e].astype(BF16)
    gate_grad = dot_nn(mix_block, ef_all[...].reshape(n_cores * n_e, n_g).astype(BF16))
    gate = gates[...]
    held_mid[c, :, : n_o + n_i] = total[:, : n_o + n_i].astype(BF16)
    held_mid[c, :, n_o + n_i :] = (gate_grad * gate * (1.0 - gate)).astype(BF16)
    for k, dev in enumerate(peers):
        send(ids.share_mid + k, held_mid.at[c], held_mid.at[c], dev)

    rs_step(3, *core_args, ids.core_z)

    for k in range(n_cores - 1):
        arrive(ids.share_mid + k, held_mid.at[peers_from(y_hi, x, n_x)[k]])
    latent = held_mid[:, :, :n_o].reshape(rows, n_o)
    pgrad = held_mid[:, :, n_o : n_o + n_i].reshape(rows, n_i)
    logit_grad = held_mid[:, :, n_o + n_i :].reshape(rows, n_g)
    blk = (2, n_z, 2)
    fac_b[:, :, :, :i_rows] = (
        (dot_tn(pgrad, tok[...]) * inv_rows).astype(BF16).reshape(*blk, i_rows, width)
    )
    fac_b[:, :, :, i_rows : 2 * i_rows] = (
        (dot_tn(latent, og[...]) * inv_rows).astype(BF16).reshape(*blk, i_rows, width)
    )
    g_rows = n_g // n_dp
    router_term = (dot_tn(logit_grad, tok[...]) * inv_rows).reshape(*blk, g_rows, width)
    expert_wide = jnp.concatenate(
        [expert_term, jnp.zeros((n_g, width - 128), F32)], axis=1
    ) if width > 128 else expert_term
    fac_b[:, :, :, 2 * i_rows :] = jnp.concatenate(
        [router_term, expert_wide.reshape(*blk, g_rows, width)], axis=3
    ).astype(BF16)
    send(ids.fac_sib, fac_b.at[:, :, 1 - core], fac_s, sib)

    rs_step(4, *core_args, ids.core_z)
    for s in range(5, steps + 1):
        rs_step(s, *core_args, ids.core_z)

    arrive(ids.fac_sib, fac_s)
    rs_step(1, *fac_args, ids.fac_z)
    rs_turn(*core_args, core_yr, ids.core_z, ids.core_y)
    mixed_ref[...] = dot_nn(latent, outf[...]).astype(BF16)
    rs_step(2, *fac_args, ids.fac_z)
    tgrad_ref[...] = (dot_nn(pgrad, inf[...]) + dot_nn(logit_grad, rw[...])).astype(BF16)
    for s in range(3, steps + 1):
        rs_step(s, *fac_args, ids.fac_z)
    cgrad_ref[...] = rs_end(*core_args, core_yr, ids.core_z, ids.core_y)
    rs_turn(*fac_args, fac_yr, ids.fac_z, ids.fac_y)
    val = rs_end(*fac_args, fac_yr, ids.fac_z, ids.fac_y)
    igrad_ref[...] = val[:i_rows]
    ograd_ref[...] = val[i_rows : 2 * i_rows]
    rgrad_ref[...] = val[2 * i_rows : 2 * i_rows + g_rows]
    egrad_ref[...] = val[2 * i_rows + g_rows :, :n_e]

    for d in sent:
        d.wait_send()

    def drain(e, _):
        pltpu.make_async_remote_copy(
            core_b.at[:, :, 1 - core, e],
            core_s.at[:, :, e],
            ss.at[ids.core_sib + e],
            rs.at[ids.core_sib + e],
            device_id=sib,
            device_id_type=MESH,
        ).wait_send()
        return 0

    lax.fori_loop(0, n_e, drain, 0)


def peers_from(y_hi, x, n_x):
    out = []
    for dy in range(2):
        for dx in range(n_x):
            if dy or dx:
                out.append(lax.rem(y_hi + dy, 2) * n_x + lax.rem(x + n_x - dx, n_x))
    return out


def shards(n_dp, n_cores, tokens, router_weight, expert_factor, input_factor, core_tensor,
           output_factor, out_grad):
    n_z = n_dp // 4
    steps = n_z // 2
    rows, width = tokens.shape
    n_g = router_weight.shape[0]
    n_i = input_factor.shape[0]
    n_o = output_factor.shape[0]
    i_rows, n_e, _ = core_tensor.shape
    g_rows = n_g // n_dp
    block = rows // n_cores
    core_in = jnp.transpose(core_tensor, (1, 0, 2))
    cblk = (n_e, i_rows, n_o)
    fblk = (2 * i_rows + 2 * g_rows, width)
    in_cols = n_g + n_i + n_o
    mid_cols = n_o + n_i + 128
    ids = Ids(n_z, n_cores, n_e)
    vmem = pltpu.VMEM
    scratch = [
        vmem((rows, width), BF16),
        vmem((n_g, width), BF16),
        vmem((n_e, n_g), BF16),
        vmem((n_i, width), BF16),
        vmem((n_o, width), BF16),
        vmem((rows, width), BF16),
        vmem((2, n_z, 2) + cblk, BF16),
        vmem((n_cores, n_e, n_g), F32),
        vmem((n_cores, block, in_cols), F32),
        vmem((n_cores - 1, block, in_cols), F32),
        vmem((n_cores, block, in_cols), BF16),
        vmem((block, n_g), F32),
        vmem((n_cores, block, mid_cols), BF16),
        vmem((n_cores - 1, block, mid_cols), BF16),
        vmem((n_cores, block, in_cols), BF16),
        vmem((n_e, rows, 128), F32),
        vmem((n_e, rows, n_o), BF16),
        vmem((rows, n_o), F32),
        vmem((rows, n_i), F32),
        vmem((rows, 128), F32),
        vmem((2, n_z, 2) + cblk, BF16),
        vmem((2, n_z) + cblk, BF16),
        vmem((2, 2, steps) + cblk, BF16),
        vmem(cblk, BF16),
        vmem((2, n_z, 2) + fblk, BF16),
        vmem((2, n_z) + fblk, BF16),
        vmem((2, 2, steps) + fblk, BF16),
        vmem(fblk, BF16),
        pltpu.SemaphoreType.DMA((7,)),
        pltpu.SemaphoreType.DMA((ids.count,)),
        pltpu.SemaphoreType.DMA((ids.count,)),
    ]
    sds = jax.ShapeDtypeStruct
    outs = pl.pallas_call(
        functools.partial(kernel, n_z, n_cores),
        out_shape=(
            sds((rows, width), BF16),
            sds((rows, width), BF16),
            sds(cblk, F32),
            sds((i_rows, width), F32),
            sds((g_rows, width), F32),
            sds((i_rows, width), F32),
            sds((g_rows, n_e), F32),
        ),
        in_specs=[pl.BlockSpec(memory_space=pl.ANY)] * 7,
        out_specs=[pl.BlockSpec(memory_space=pltpu.VMEM)] * 7,
        scratch_shapes=scratch,
        compiler_params=pltpu.CompilerParams(
            collective_id=0, has_side_effects=True, vmem_limit_bytes=56 * 1024 * 1024
        ),
    )(tokens, router_weight, expert_factor.T, input_factor, core_in, output_factor, out_grad)
    mixed, tgrad, cgrad, igrad, rgrad, ograd, egrad = outs
    return mixed, tgrad, jnp.transpose(cgrad, (1, 0, 2)), igrad, rgrad, ograd, egrad


def solution(mesh):
    return jax.shard_map(
        functools.partial(shards, mesh.shape["dp"], mesh.shape["cores"]),
        mesh=mesh,
        in_specs=(
            P("dp", "cores"),
            P(None, "cores"),
            P(None, "cores"),
            P(None, "cores"),
            P("dp", "cores", None),
            P(None, "cores"),
            P("dp", "cores"),
        ),
        out_specs=(
            P("dp", "cores"),
            P("dp", "cores"),
            P("dp", "cores", None),
            P("dp", "cores"),
            P("dp", "cores"),
            P("dp", "cores"),
            P("dp", "cores"),
        ),
        check_vma=False,
    )
```

```python
import functools

import jax
import jax.numpy as jnp
from jax import lax
from jax.experimental import pallas as pl
from jax.experimental.pallas import tpu as pltpu
from jax.sharding import PartitionSpec as P

MESH = pl.DeviceIdType.MESH
F32 = jnp.float32
BF16 = jnp.bfloat16


def dot_nn(a, b):
    return lax.dot_general(a, b, (((1,), (0,)), ((), ())), preferred_element_type=F32)


def dot_nt(a, b):
    return lax.dot_general(a, b, (((1,), (1,)), ((), ())), preferred_element_type=F32)


def dot_tn(a, b):
    return lax.dot_general(a, b, (((0,), (0,)), ((), ())), preferred_element_type=F32)


def ring_hops(n_z):
    up = n_z // 2
    down = n_z - 1 - up
    return ((up, down), (down, up))


class Ids:
    def __init__(self, n_z, n_cores, n_e):
        self.count = 0
        steps = n_z // 2
        self.gather_y = self.take(1)
        self.gather_z = self.take(4 * steps)
        self.gather_sib = self.take(2 * n_z)
        self.factor = self.take(n_cores - 1)
        self.sum_in = self.take(2 * (n_cores - 1))
        self.share_in = self.take(2 * (n_cores - 1))
        self.sum_mid = self.take(2 * (n_cores - 1))
        self.share_mid = self.take(2 * (n_cores - 1))
        self.core_sib = self.take(n_e)
        self.core_z = self.take(4 * steps)
        self.core_y = self.take(1)
        self.out_sib = self.take(1)
        self.out_z = self.take(4 * steps)
        self.out_y = self.take(1)
        self.inp_sib = self.take(1)
        self.inp_z = self.take(4 * steps)
        self.inp_y = self.take(1)

    def take(self, n):
        first = self.count
        self.count += n
        return first


def kernel(
    n_z, n_cores,
    tok_hbm, rw_hbm, ef_hbm, inf_hbm, core_hbm, outf_hbm, og_hbm,
    mixed_ref, tgrad_ref, cgrad_ref, igrad_ref, rgrad_ref, ograd_ref, egrad_ref,
    mixed_v, tgrad_v, cgrad_v, igrad_v, rgrad_v, ograd_v, egrad_v,
    tok, rw, ef, inf, outf, og, core_v,
    whole, ef_all, part_in, got_in, held_in, gates, part_mid, got_mid, held_mid,
    mix_b, outer, lat_acc, pg_acc, mg_acc,
    core_b, core_s, core_r, core_yr,
    fac_b, fac_s, fac_r, fac_yr,
    inp_b, inp_s, inp_r, inp_yr,
    in_sem, out_sem, ss, rs,
):
    rows, width = tok.shape
    n_g = rw.shape[0]
    n_i = inf.shape[0]
    n_o = outf.shape[0]
    n_e = ef.shape[0]
    block = rows // n_cores
    i_rows = whole.shape[4]
    n_dp = 4 * n_z
    inv_rows = 1.0 / rows
    ids = Ids(n_z, n_cores, n_e)
    steps = n_z // 2
    hops = ring_hops(n_z)

    dp = lax.axis_index("dp")
    c = lax.axis_index("cores")
    core = lax.rem(dp, 2)
    z = lax.rem(dp // 2, n_z)
    y = dp // (2 * n_z)

    def at(yy, zz, kk):
        return ((yy * n_z + zz) * 2 + kk, c)

    def zmod(offset):
        return lax.rem(z + offset + 2 * n_z, n_z)

    sib = at(y, z, 1 - core)
    ynb = at(1 - y, z, core)
    znb = (at(y, zmod(1), core), at(y, zmod(-1), core))
    n_x = n_cores // 2
    y_hi = c // n_x
    x = lax.rem(c, n_x)
    peers = []
    for dy in range(2):
        for dx in range(n_x):
            if dy or dx:
                other = lax.rem(y_hi + dy, 2) * n_x + lax.rem(x + dx, n_x)
                peers.append((dp, other))

    sent = []

    def send(i, src, dst, dev):
        d = pltpu.make_async_remote_copy(
            src, dst, ss.at[i], rs.at[i], device_id=dev, device_id_type=MESH
        )
        d.start()
        sent.append(d)

    def arrive(i, ref):
        pltpu.make_async_remote_copy(
            ref, ref, ss.at[i], rs.at[i], device_id=sib, device_id_type=MESH
        ).wait_recv()

    loads = [
        pltpu.make_async_copy(src, dst, in_sem.at[n])
        for n, (src, dst) in enumerate(
            (
                (core_hbm, core_v),
                (og_hbm, og),
                (outf_hbm, outf),
                (tok_hbm, tok),
                (inf_hbm, inf),
                (rw_hbm, rw),
                (ef_hbm, ef),
            )
        )
    ]
    for load in loads:
        load.start()

    barrier = pltpu.get_barrier_semaphore()
    greet = [sib, ynb, znb[0], znb[1]] + peers
    for dev in greet:
        pl.semaphore_signal(barrier, inc=1, device_id=dev, device_id_type=MESH)
    loads[0].wait()
    whole[y, z, core] = jnp.swapaxes(core_v[...].astype(F32), 0, 1).astype(BF16)
    pl.semaphore_wait(barrier, len(greet))

    lane_y = (y, 1 - y)

    def ag_id(lane, way, s):
        return ids.gather_z + (lane * 2 + way) * steps + s - 1

    def ag_ref(lane, zz):
        return whole.at[lane_y[lane], zz, core]

    def ag_sib(lane, offset):
        ref = ag_ref(lane, zmod(offset))
        send(ids.gather_sib + lane * n_z + offset % n_z, ref, ref, sib)

    def ag_open(lane):
        ref = ag_ref(lane, z)
        for way in range(2):
            if hops[lane][way] >= 1:
                send(ag_id(lane, way, 1), ref, ref, znb[way])
        ag_sib(lane, 0)

    def ag_step(s, lane):
        for way in range(2):
            if s <= hops[lane][way]:
                offset = -s if way == 0 else s
                ref = ag_ref(lane, zmod(offset))
                arrive(ag_id(lane, way, s), ref)
                if s + 1 <= hops[lane][way]:
                    send(ag_id(lane, way, s + 1), ref, ref, znb[way])
                ag_sib(lane, offset)

    def ag_close():
        for lane in range(2):
            for offset in range(n_z):
                ref = whole.at[lane_y[lane], zmod(offset), 1 - core]
                arrive(ids.gather_sib + lane * n_z + offset, ref)

    behind = peers_from(y_hi, x, n_x)
    n_peers = n_cores - 1

    def sum_send(first, src, got, cols):
        for k, dev in enumerate(peers):
            send(first + k, src.at[dev[1], :, cols], got.at[k, :, cols], dev)

    def sum_wait(first, src, got, cols):
        for k in range(n_peers):
            arrive(first + k, got.at[k, :, cols])
        total = src[c, :, cols].astype(F32)
        for k in range(n_peers):
            total = total + got[k, :, cols].astype(F32)
        return total

    def share_send(first, held, cols):
        for k, dev in enumerate(peers):
            send(first + k, held.at[c, :, cols], held.at[c, :, cols], dev)

    def share_wait(first, held, cols):
        for k in range(n_peers):
            arrive(first + k, held.at[behind[k], :, cols])

    send(ids.gather_y, ag_ref(0, z), ag_ref(0, z), ynb)
    ag_open(0)

    n_gi = n_g + n_i
    gi = slice(0, n_gi)
    out_cols = slice(n_gi, n_gi + n_o)
    loads[1].wait()
    loads[2].wait()
    part_in[:, :, out_cols] = dot_nt(og[...], outf[...]).reshape(n_cores, block, n_o)
    sum_send(ids.sum_in, part_in, got_in, out_cols)
    loads[3].wait()
    loads[4].wait()
    part_in[:, :, n_g:n_gi] = dot_nt(tok[...], inf[...]).reshape(n_cores, block, n_i)
    loads[5].wait()
    part_in[:, :, :n_g] = dot_nt(tok[...], rw[...]).reshape(n_cores, block, n_g)
    sum_send(ids.sum_in + n_peers, part_in, got_in, gi)
    loads[6].wait()
    ef_all[c] = ef[...].astype(F32)
    for k, dev in enumerate(peers):
        send(ids.factor + k, ef_all.at[c], ef_all.at[c], dev)

    arrive(ids.gather_y, ag_ref(1, z))
    ag_open(1)
    ag_step(1, 0)
    ag_step(1, 1)

    held_in[c, :, out_cols] = sum_wait(ids.sum_in, part_in, got_in, out_cols).astype(BF16)
    share_send(ids.share_in, held_in, out_cols)

    ag_step(2, 0)
    ag_step(2, 1)
    ag_step(3, 0)

    total = sum_wait(ids.sum_in + n_peers, part_in, got_in, gi)
    gate = jax.nn.sigmoid(total[:, :n_g])
    gates[...] = gate
    held_in[c, :, :n_g] = gate.astype(BF16)
    held_in[c, :, n_g:n_gi] = total[:, n_g:].astype(BF16)
    share_send(ids.share_in + n_peers, held_in, gi)

    ag_step(3, 1)
    for s in range(4, steps + 1):
        ag_step(s, 0)
        ag_step(s, 1)

    share_wait(ids.share_in, held_in, out_cols)
    lgrad = held_in[:, :, out_cols].reshape(rows, n_o)
    lgrad_wide = lgrad.astype(F32)
    share_wait(ids.share_in + n_peers, held_in, gi)
    gate_low = held_in[:, :, :n_g].reshape(rows, n_g)
    proj = held_in[:, :, n_g:n_gi].reshape(rows, n_i)
    mixing = dot_nt(gate_low, ef[...])
    for e in range(n_e):
        mix_b[e] = jnp.broadcast_to(mixing[:, e : e + 1], (rows, 128))

    def wide(v, n):
        return jnp.concatenate([v] * (n // 128), axis=1)

    proj_t = proj.T

    def core_sib(e):
        return pltpu.make_async_remote_copy(
            core_b.at[:, :, 1 - core, e],
            core_s.at[:, :, e],
            ss.at[ids.core_sib + e],
            rs.at[ids.core_sib + e],
            device_id=sib,
            device_id_type=MESH,
        )

    def core_terms(e, _):
        o = (wide(mix_b[e], n_o) * lgrad_wide).astype(BF16)
        outer[e] = o
        term = dot_nn(proj_t, o) * inv_rows
        core_b[:, :, :, e] = term.astype(BF16).reshape(2, n_z, 2, i_rows, n_o)
        core_sib(e).start()
        return 0

    lax.fori_loop(0, n_e, core_terms, 0)

    def rs_step(s, src, sib_got, got, first):
        for lane in range(2):
            for way in range(2):
                k = hops[lane][way]
                if s <= k:
                    far = k - s + 1
                    d = zmod(far if way == 0 else -far)
                    val = src[lane_y[lane], d, core].astype(F32) + sib_got[
                        lane_y[lane], d
                    ].astype(F32)
                    if s > 1:
                        arrive(first + (lane * 2 + way) * steps + s - 2, got.at[lane, way, s - 2])
                        val = val + got[lane, way, s - 2].astype(F32)
                    src[lane_y[lane], d, core] = val.astype(BF16)
                    send(
                        first + (lane * 2 + way) * steps + s - 1,
                        src.at[lane_y[lane], d, core],
                        got.at[lane, way, s - 1],
                        znb[way],
                    )

    def rs_lane(lane, src, sib_got, got, first):
        val = src[lane_y[lane], z, core].astype(F32) + sib_got[lane_y[lane], z].astype(F32)
        for way in range(2):
            k = hops[lane][way]
            if k:
                arrive(first + (lane * 2 + way) * steps + k - 1, got.at[lane, way, k - 1])
                val = val + got[lane, way, k - 1].astype(F32)
        return val

    def rs_turn(src, sib_got, got, yr, first, y_id):
        val = rs_lane(1, src, sib_got, got, first)
        src[1 - y, z, core] = val.astype(BF16)
        send(y_id, src.at[1 - y, z, core], yr, ynb)

    def rs_end(src, sib_got, got, yr, first, y_id):
        val = rs_lane(0, src, sib_got, got, first)
        arrive(y_id, yr)
        return val + yr[...].astype(F32)

    core_args = (core_b, core_s, core_r)
    fac_o = (fac_b, fac_s, fac_r)
    fac_i = (inp_b, inp_s, inp_r)

    ag_close()

    lat_acc[...] = jnp.zeros_like(lat_acc)
    pg_acc[...] = jnp.zeros_like(pg_acc)
    mg_acc[...] = jnp.zeros_like(mg_acc)
    lane_no = lax.broadcasted_iota(jnp.int32, (rows, 128), 1)

    def forward(e, _):
        expanded = dot_nn(proj, whole[:, :, :, e].reshape(n_i, n_o))
        lat_acc[...] += wide(mix_b[e], n_o) * expanded
        col = jnp.sum(lgrad_wide * expanded, axis=1, keepdims=True)
        mg_acc[...] += jnp.where(lane_no == c * n_e + e, col, 0.0)
        return 0

    def backward(e, _):
        pg_acc[...] += dot_nt(outer[e], whole[:, :, :, e].reshape(n_i, n_o))
        return 0

    n_om = n_o + 128
    lat_mix = slice(0, n_om)
    pg_cols = slice(n_om, n_om + n_i)
    lax.fori_loop(0, n_e, forward, 0)
    part_mid[:, :, :n_o] = lat_acc[...].astype(BF16).reshape(n_cores, block, n_o)
    mix_low = mg_acc[...].astype(BF16)
    part_mid[:, :, n_o:n_om] = mix_low.reshape(n_cores, block, 128)
    sum_send(ids.sum_mid, part_mid, got_mid, lat_mix)

    for e in range(n_e):
        arrive(ids.core_sib + e, core_s.at[:, :, e])
    rs_step(1, *core_args, ids.core_z)

    lax.fori_loop(0, n_e, backward, 0)
    part_mid[:, :, pg_cols] = pg_acc[...].astype(BF16).reshape(n_cores, block, n_i)
    sum_send(ids.sum_mid + n_peers, part_mid, got_mid, pg_cols)

    expert_full = dot_tn(gate_low, mix_low) * inv_rows
    pick = (
        lax.broadcasted_iota(jnp.int32, (128, 128), 0)
        == lax.broadcasted_iota(jnp.int32, (128, 128), 1) + c * n_e
    ).astype(BF16)
    expert_term = dot_nn(expert_full.astype(BF16), pick)

    for k in range(n_peers):
        arrive(ids.factor + k, ef_all.at[behind[k]])
    total = sum_wait(ids.sum_mid, part_mid, got_mid, lat_mix)
    mix_block = total[:, n_o : n_o + n_cores * n_e].astype(BF16)
    gate_grad = dot_nn(mix_block, ef_all[...].reshape(n_cores * n_e, n_g).astype(BF16))
    gate = gates[...]
    n_og = n_o + n_g
    lat_logit = slice(0, n_og)
    pg_held = slice(n_og, n_og + n_i)
    held_mid[c, :, :n_o] = total[:, :n_o].astype(BF16)
    held_mid[c, :, n_o:n_og] = (gate_grad * gate * (1.0 - gate)).astype(BF16)
    share_send(ids.share_mid, held_mid, lat_logit)

    rs_step(2, *core_args, ids.core_z)

    held_mid[c, :, pg_held] = sum_wait(
        ids.sum_mid + n_peers, part_mid, got_mid, pg_cols
    ).astype(BF16)
    share_send(ids.share_mid + n_peers, held_mid, pg_held)

    share_wait(ids.share_mid, held_mid, lat_logit)
    latent = held_mid[:, :, :n_o].reshape(rows, n_o)
    logit_grad = held_mid[:, :, n_o:n_og].reshape(rows, n_g)
    blk = (2, n_z, 2)
    g_rows = n_g // n_dp
    fac_b[:, :, :, :i_rows] = (
        (dot_tn(latent, og[...]) * inv_rows).astype(BF16).reshape(*blk, i_rows, width)
    )
    router_term = (dot_tn(logit_grad, tok[...]) * inv_rows).reshape(*blk, g_rows, width)
    expert_wide = jnp.concatenate(
        [expert_term, jnp.zeros((n_g, width - 128), F32)], axis=1
    ) if width > 128 else expert_term
    fac_b[:, :, :, i_rows:] = jnp.concatenate(
        [router_term, expert_wide.reshape(*blk, g_rows, width)], axis=3
    ).astype(BF16)
    send(ids.out_sib, fac_b.at[:, :, 1 - core], fac_s, sib)

    rs_step(3, *core_args, ids.core_z)

    arrive(ids.out_sib, fac_s)
    rs_step(1, *fac_o, ids.out_z)

    share_wait(ids.share_mid + n_peers, held_mid, pg_held)
    pgrad = held_mid[:, :, pg_held].reshape(rows, n_i)
    inp_b[...] = (dot_tn(pgrad, tok[...]) * inv_rows).astype(BF16).reshape(*blk, i_rows, width)
    send(ids.inp_sib, inp_b.at[:, :, 1 - core], inp_s, sib)

    for s in range(4, steps + 1):
        rs_step(s, *core_args, ids.core_z)
    arrive(ids.inp_sib, inp_s)
    rs_step(1, *fac_i, ids.inp_z)
    rs_step(2, *fac_o, ids.out_z)

    mixed_v[...] = dot_nn(latent, outf[...]).astype(BF16)
    results = [pltpu.make_async_copy(mixed_v, mixed_ref, out_sem.at[0])]
    results[0].start()

    rs_turn(*core_args, core_yr, ids.core_z, ids.core_y)
    rs_step(2, *fac_i, ids.inp_z)
    rs_step(3, *fac_o, ids.out_z)
    tgrad_v[...] = (dot_nn(pgrad, inf[...]) + dot_nn(logit_grad, rw[...])).astype(BF16)

    def result(src, dst):
        results.append(pltpu.make_async_copy(src, dst, out_sem.at[len(results)]))
        results[-1].start()

    result(tgrad_v, tgrad_ref)
    rs_step(3, *fac_i, ids.inp_z)
    for s in range(4, steps + 1):
        rs_step(s, *fac_o, ids.out_z)
        rs_step(s, *fac_i, ids.inp_z)
    rs_turn(*fac_o, fac_yr, ids.out_z, ids.out_y)
    rs_turn(*fac_i, inp_yr, ids.inp_z, ids.inp_y)
    cgrad_v[...] = jnp.swapaxes(rs_end(*core_args, core_yr, ids.core_z, ids.core_y), 0, 1)
    result(cgrad_v, cgrad_ref)
    val = rs_end(*fac_o, fac_yr, ids.out_z, ids.out_y)
    ograd_v[...] = val[:i_rows]
    rgrad_v[...] = val[i_rows : i_rows + g_rows]
    egrad_v[...] = val[i_rows + g_rows :, :n_e]
    result(ograd_v, ograd_ref)
    result(rgrad_v, rgrad_ref)
    result(egrad_v, egrad_ref)
    igrad_v[...] = rs_end(*fac_i, inp_yr, ids.inp_z, ids.inp_y)
    result(igrad_v, igrad_ref)

    for d in sent:
        d.wait_send()

    def drain(e, _):
        core_sib(e).wait_send()
        return 0

    lax.fori_loop(0, n_e, drain, 0)
    for r in results:
        r.wait()


def hand_over(*refs):
    n = len(refs) // 2
    sems = refs[-1]
    copies = [pltpu.make_async_copy(refs[i], refs[n + i], sems.at[i]) for i in range(n)]
    for copy in copies:
        copy.start()
    for copy in copies:
        copy.wait()


def peers_from(y_hi, x, n_x):
    out = []
    for dy in range(2):
        for dx in range(n_x):
            if dy or dx:
                out.append(lax.rem(y_hi + dy, 2) * n_x + lax.rem(x + n_x - dx, n_x))
    return out


def shards(n_dp, n_cores, tokens, router_weight, expert_factor, input_factor, core_tensor,
           output_factor, out_grad):
    n_z = n_dp // 4
    steps = n_z // 2
    rows, width = tokens.shape
    n_g = router_weight.shape[0]
    n_i = input_factor.shape[0]
    n_o = output_factor.shape[0]
    i_rows, n_e, _ = core_tensor.shape
    g_rows = n_g // n_dp
    block = rows // n_cores
    cblk = (n_e, i_rows, n_o)
    fblk = (i_rows + 2 * g_rows, width)
    iblk = (i_rows, width)
    in_cols = n_g + n_i + n_o
    mid_cols = n_o + n_i + 128
    ids = Ids(n_z, n_cores, n_e)
    sds = jax.ShapeDtypeStruct
    results = (
        sds((rows, width), BF16),
        sds((rows, width), BF16),
        sds((i_rows, n_e, n_o), F32),
        sds((i_rows, width), F32),
        sds((g_rows, width), F32),
        sds((i_rows, width), F32),
        sds((g_rows, n_e), F32),
    )
    vmem = pltpu.VMEM
    scratch = [vmem(r.shape, r.dtype) for r in results] + [
        vmem((rows, width), BF16),
        vmem((n_g, width), BF16),
        vmem((n_e, n_g), BF16),
        vmem((n_i, width), BF16),
        vmem((n_o, width), BF16),
        vmem((rows, width), BF16),
        vmem((i_rows, n_e, n_o), BF16),
        vmem((2, n_z, 2) + cblk, BF16),
        vmem((n_cores, n_e, n_g), F32),
        vmem((n_cores, block, in_cols), F32),
        vmem((n_cores - 1, block, in_cols), F32),
        vmem((n_cores, block, in_cols), BF16),
        vmem((block, n_g), F32),
        vmem((n_cores, block, mid_cols), BF16),
        vmem((n_cores - 1, block, mid_cols), BF16),
        vmem((n_cores, block, in_cols), BF16),
        vmem((n_e, rows, 128), F32),
        vmem((n_e, rows, n_o), BF16),
        vmem((rows, n_o), F32),
        vmem((rows, n_i), F32),
        vmem((rows, 128), F32),
        vmem((2, n_z, 2) + cblk, BF16),
        vmem((2, n_z) + cblk, BF16),
        vmem((2, 2, steps) + cblk, BF16),
        vmem(cblk, BF16),
        vmem((2, n_z, 2) + fblk, BF16),
        vmem((2, n_z) + fblk, BF16),
        vmem((2, 2, steps) + fblk, BF16),
        vmem(fblk, BF16),
        vmem((2, n_z, 2) + iblk, BF16),
        vmem((2, n_z) + iblk, BF16),
        vmem((2, 2, steps) + iblk, BF16),
        vmem(iblk, BF16),
        pltpu.SemaphoreType.DMA((7,)),
        pltpu.SemaphoreType.DMA((7,)),
        pltpu.SemaphoreType.DMA((ids.count,)),
        pltpu.SemaphoreType.DMA((ids.count,)),
    ]
    outs = pl.pallas_call(
        functools.partial(kernel, n_z, n_cores),
        out_shape=results,
        in_specs=[pl.BlockSpec(memory_space=pl.ANY)] * 7,
        out_specs=[pl.BlockSpec(memory_space=pl.ANY)] * 7,
        scratch_shapes=scratch,
        compiler_params=pltpu.CompilerParams(
            collective_id=0, has_side_effects=True, vmem_limit_bytes=56 * 1024 * 1024
        ),
    )(tokens, router_weight, expert_factor.T, input_factor, core_tensor, output_factor, out_grad)
    return pl.pallas_call(
        hand_over,
        out_shape=results,
        in_specs=[pl.BlockSpec(memory_space=pl.ANY)] * 7,
        out_specs=[pl.BlockSpec(memory_space=pl.ANY)] * 7,
        scratch_shapes=[pltpu.SemaphoreType.DMA((7,))],
    )(*outs)


def solution(mesh):
    return jax.shard_map(
        functools.partial(shards, mesh.shape["dp"], mesh.shape["cores"]),
        mesh=mesh,
        in_specs=(
            P("dp", "cores"),
            P(None, "cores"),
            P(None, "cores"),
            P(None, "cores"),
            P("dp", "cores", None),
            P(None, "cores"),
            P("dp", "cores"),
        ),
        out_specs=(
            P("dp", "cores"),
            P("dp", "cores"),
            P("dp", "cores", None),
            P("dp", "cores"),
            P("dp", "cores"),
            P("dp", "cores"),
            P("dp", "cores"),
        ),
        check_vma=False,
    )
```

```python
import functools

import jax
import jax.numpy as jnp
from jax import lax
from jax.experimental import pallas as pl
from jax.experimental.pallas import tpu as pltpu
from jax.sharding import PartitionSpec as P

MESH = pl.DeviceIdType.MESH
F32 = jnp.float32
BF16 = jnp.bfloat16


def dot_nn(a, b):
    return lax.dot_general(a, b, (((1,), (0,)), ((), ())), preferred_element_type=F32)


def dot_nt(a, b):
    return lax.dot_general(a, b, (((1,), (1,)), ((), ())), preferred_element_type=F32)


def dot_tn(a, b):
    return lax.dot_general(a, b, (((0,), (0,)), ((), ())), preferred_element_type=F32)


def ring_hops(n_z):
    up = n_z // 2
    down = n_z - 1 - up
    return ((up, down), (down, up))


class Ids:
    def __init__(self, n_z, n_cores, n_e):
        self.count = 0
        steps = n_z // 2
        self.gather_y = self.take(1)
        self.gather_z = self.take(4 * steps)
        self.gather_sib = self.take(2 * n_z)
        self.factor = self.take(n_cores - 1)
        self.sum_in = self.take(2 * (n_cores - 1))
        self.share_in = self.take(2 * (n_cores - 1))
        self.sum_mid = self.take(2 * (n_cores - 1))
        self.share_mid = self.take(2 * (n_cores - 1))
        self.core_sib = self.take(n_e)
        self.core_z = self.take(4 * steps)
        self.core_y = self.take(1)
        self.out_sib = self.take(1)
        self.out_z = self.take(4 * steps)
        self.out_y = self.take(1)
        self.inp_sib = self.take(1)
        self.inp_z = self.take(4 * steps)
        self.inp_y = self.take(1)

    def take(self, n):
        first = self.count
        self.count += n
        return first


def kernel(
    n_z, n_cores,
    tok_hbm, rw_hbm, ef_hbm, inf_hbm, core_hbm, outf_hbm, og_hbm,
    mixed_ref, tgrad_ref, cgrad_ref, igrad_ref, rgrad_ref, ograd_ref, egrad_ref,
    mixed_v, tgrad_v, cgrad_v, igrad_v, rgrad_v, ograd_v, egrad_v,
    tok, rw, ef, inf, outf, og, core_v,
    whole, ef_all, part_in, got_in, held_in, gates, part_mid, got_mid, held_mid,
    mix_b, outer, lat_acc, pg_acc, mg_acc,
    core_b, core_s, core_r, core_yr,
    fac_b, fac_s, fac_r, fac_yr,
    inp_b, inp_s, inp_r, inp_yr,
    in_sem, out_sem, ss, rs,
):
    rows, width = tok.shape
    n_g = rw.shape[0]
    n_i = inf.shape[0]
    n_o = outf.shape[0]
    n_e = ef.shape[0]
    block = rows // n_cores
    i_rows = whole.shape[4]
    n_dp = 4 * n_z
    inv_rows = 1.0 / rows
    ids = Ids(n_z, n_cores, n_e)
    steps = n_z // 2
    hops = ring_hops(n_z)

    dp = lax.axis_index("dp")
    c = lax.axis_index("cores")
    core = lax.rem(dp, 2)
    z = lax.rem(dp // 2, n_z)
    y = dp // (2 * n_z)

    def at(yy, zz, kk):
        return ((yy * n_z + zz) * 2 + kk, c)

    def zmod(offset):
        return lax.rem(z + offset + 2 * n_z, n_z)

    sib = at(y, z, 1 - core)
    ynb = at(1 - y, z, core)
    znb = (at(y, zmod(1), core), at(y, zmod(-1), core))
    n_x = n_cores // 2
    y_hi = c // n_x
    x = lax.rem(c, n_x)
    peers = []
    for dy in range(2):
        for dx in range(n_x):
            if dy or dx:
                other = lax.rem(y_hi + dy, 2) * n_x + lax.rem(x + dx, n_x)
                peers.append((dp, other))

    sent = []

    def send(i, src, dst, dev):
        d = pltpu.make_async_remote_copy(
            src, dst, ss.at[i], rs.at[i], device_id=dev, device_id_type=MESH
        )
        d.start()
        sent.append(d)

    def arrive(i, ref):
        pltpu.make_async_remote_copy(
            ref, ref, ss.at[i], rs.at[i], device_id=sib, device_id_type=MESH
        ).wait_recv()

    loads = [
        pltpu.make_async_copy(src, dst, in_sem.at[n])
        for n, (src, dst) in enumerate(
            (
                (core_hbm, core_v),
                (og_hbm, og),
                (outf_hbm, outf),
                (tok_hbm, tok),
                (inf_hbm, inf),
                (rw_hbm, rw),
                (ef_hbm, ef),
            )
        )
    ]
    for load in loads:
        load.start()

    barrier = pltpu.get_barrier_semaphore()
    greet = [sib, ynb, znb[0], znb[1]] + peers
    for dev in greet:
        pl.semaphore_signal(barrier, inc=1, device_id=dev, device_id_type=MESH)
    loads[0].wait()
    whole[y, z, core] = jnp.swapaxes(core_v[...].astype(F32), 0, 1).astype(BF16)
    pl.semaphore_wait(barrier, len(greet))

    lane_y = (y, 1 - y)

    def ag_id(lane, way, s):
        return ids.gather_z + (lane * 2 + way) * steps + s - 1

    def ag_ref(lane, zz):
        return whole.at[lane_y[lane], zz, core]

    def ag_sib(lane, offset):
        ref = ag_ref(lane, zmod(offset))
        send(ids.gather_sib + lane * n_z + offset % n_z, ref, ref, sib)

    def ag_open(lane):
        ref = ag_ref(lane, z)
        for way in range(2):
            if hops[lane][way] >= 1:
                send(ag_id(lane, way, 1), ref, ref, znb[way])
        ag_sib(lane, 0)

    def ag_step(s, lane):
        for way in range(2):
            if s <= hops[lane][way]:
                offset = -s if way == 0 else s
                ref = ag_ref(lane, zmod(offset))
                arrive(ag_id(lane, way, s), ref)
                if s + 1 <= hops[lane][way]:
                    send(ag_id(lane, way, s + 1), ref, ref, znb[way])
                ag_sib(lane, offset)

    def ag_close():
        for lane in range(2):
            for offset in range(n_z):
                ref = whole.at[lane_y[lane], zmod(offset), 1 - core]
                arrive(ids.gather_sib + lane * n_z + offset, ref)

    behind = peers_from(y_hi, x, n_x)
    n_peers = n_cores - 1

    def sum_send(first, src, got, cols):
        for k, dev in enumerate(peers):
            send(first + k, src.at[dev[1], :, cols], got.at[k, :, cols], dev)

    def sum_wait(first, src, got, cols):
        for k in range(n_peers):
            arrive(first + k, got.at[k, :, cols])
        total = src[c, :, cols].astype(F32)
        for k in range(n_peers):
            total = total + got[k, :, cols].astype(F32)
        return total

    def share_send(first, held, cols):
        for k, dev in enumerate(peers):
            send(first + k, held.at[c, :, cols], held.at[c, :, cols], dev)

    def share_wait(first, held, cols):
        for k in range(n_peers):
            arrive(first + k, held.at[behind[k], :, cols])

    send(ids.gather_y, ag_ref(0, z), ag_ref(0, z), ynb)
    ag_open(0)

    n_gi = n_g + n_i
    gi = slice(0, n_gi)
    out_cols = slice(n_gi, n_gi + n_o)
    loads[1].wait()
    loads[2].wait()
    part_in[:, :, out_cols] = dot_nt(og[...], outf[...]).reshape(n_cores, block, n_o)
    sum_send(ids.sum_in, part_in, got_in, out_cols)
    loads[3].wait()
    loads[4].wait()
    part_in[:, :, n_g:n_gi] = dot_nt(tok[...], inf[...]).reshape(n_cores, block, n_i)
    loads[5].wait()
    part_in[:, :, :n_g] = dot_nt(tok[...], rw[...]).reshape(n_cores, block, n_g)
    sum_send(ids.sum_in + n_peers, part_in, got_in, gi)
    loads[6].wait()
    ef_all[c] = ef[...].astype(F32)
    for k, dev in enumerate(peers):
        send(ids.factor + k, ef_all.at[c], ef_all.at[c], dev)

    arrive(ids.gather_y, ag_ref(1, z))
    ag_open(1)
    ag_step(1, 0)
    ag_step(1, 1)

    held_in[c, :, out_cols] = sum_wait(ids.sum_in, part_in, got_in, out_cols).astype(BF16)
    share_send(ids.share_in, held_in, out_cols)

    ag_step(2, 0)
    ag_step(2, 1)
    ag_step(3, 0)

    total = sum_wait(ids.sum_in + n_peers, part_in, got_in, gi)
    gate = jax.nn.sigmoid(total[:, :n_g])
    gates[...] = gate
    held_in[c, :, :n_g] = gate.astype(BF16)
    held_in[c, :, n_g:n_gi] = total[:, n_g:].astype(BF16)
    share_send(ids.share_in + n_peers, held_in, gi)

    ag_step(3, 1)
    for s in range(4, steps + 1):
        ag_step(s, 0)
        ag_step(s, 1)

    share_wait(ids.share_in, held_in, out_cols)
    lgrad = held_in[:, :, out_cols].reshape(rows, n_o)
    lgrad_wide = lgrad.astype(F32)
    share_wait(ids.share_in + n_peers, held_in, gi)
    gate_low = held_in[:, :, :n_g].reshape(rows, n_g)
    proj = held_in[:, :, n_g:n_gi].reshape(rows, n_i)
    mixing = dot_nt(gate_low, ef[...])
    for e in range(n_e):
        mix_b[e] = jnp.broadcast_to(mixing[:, e : e + 1], (rows, 128))

    def wide(v, n):
        return jnp.concatenate([v] * (n // 128), axis=1)

    proj_t = proj.T

    def core_sib(e):
        return pltpu.make_async_remote_copy(
            core_b.at[:, :, 1 - core, e],
            core_s.at[:, :, e],
            ss.at[ids.core_sib + e],
            rs.at[ids.core_sib + e],
            device_id=sib,
            device_id_type=MESH,
        )

    def core_terms(e, _):
        o = (wide(mix_b[e], n_o) * lgrad_wide).astype(BF16)
        outer[e] = o
        term = dot_nn(proj_t, o) * inv_rows
        core_b[:, :, :, e] = term.astype(BF16).reshape(2, n_z, 2, i_rows, n_o)
        core_sib(e).start()
        return 0

    lax.fori_loop(0, n_e, core_terms, 0)

    def rs_step(s, src, sib_got, got, first):
        for lane in range(2):
            for way in range(2):
                k = hops[lane][way]
                if s <= k:
                    far = k - s + 1
                    d = zmod(far if way == 0 else -far)
                    val = src[lane_y[lane], d, core].astype(F32) + sib_got[
                        lane_y[lane], d
                    ].astype(F32)
                    if s > 1:
                        arrive(first + (lane * 2 + way) * steps + s - 2, got.at[lane, way, s - 2])
                        val = val + got[lane, way, s - 2].astype(F32)
                    src[lane_y[lane], d, core] = val.astype(BF16)
                    send(
                        first + (lane * 2 + way) * steps + s - 1,
                        src.at[lane_y[lane], d, core],
                        got.at[lane, way, s - 1],
                        znb[way],
                    )

    def rs_lane(lane, src, sib_got, got, first):
        val = src[lane_y[lane], z, core].astype(F32) + sib_got[lane_y[lane], z].astype(F32)
        for way in range(2):
            k = hops[lane][way]
            if k:
                arrive(first + (lane * 2 + way) * steps + k - 1, got.at[lane, way, k - 1])
                val = val + got[lane, way, k - 1].astype(F32)
        return val

    def rs_turn(src, sib_got, got, yr, first, y_id):
        val = rs_lane(1, src, sib_got, got, first)
        src[1 - y, z, core] = val.astype(BF16)
        send(y_id, src.at[1 - y, z, core], yr, ynb)

    def rs_end(src, sib_got, got, yr, first, y_id):
        val = rs_lane(0, src, sib_got, got, first)
        arrive(y_id, yr)
        return val + yr[...].astype(F32)

    core_args = (core_b, core_s, core_r)
    fac_o = (fac_b, fac_s, fac_r)
    fac_i = (inp_b, inp_s, inp_r)

    ag_close()

    lat_acc[...] = jnp.zeros_like(lat_acc)
    pg_acc[...] = jnp.zeros_like(pg_acc)
    mg_acc[...] = jnp.zeros_like(mg_acc)
    lane_no = lax.broadcasted_iota(jnp.int32, (rows, 128), 1)

    def forward(e, _):
        expanded = dot_nn(proj, whole[:, :, :, e].reshape(n_i, n_o))
        lat_acc[...] += wide(mix_b[e], n_o) * expanded
        col = jnp.sum(lgrad_wide * expanded, axis=1, keepdims=True)
        mg_acc[...] += jnp.where(lane_no == c * n_e + e, col, 0.0)
        return 0

    def backward(e, _):
        pg_acc[...] += dot_nt(outer[e], whole[:, :, :, e].reshape(n_i, n_o))
        return 0

    n_om = n_o + 128
    lat_mix = slice(0, n_om)
    pg_cols = slice(n_om, n_om + n_i)
    lax.fori_loop(0, n_e, forward, 0)
    part_mid[:, :, :n_o] = lat_acc[...].astype(BF16).reshape(n_cores, block, n_o)
    mix_low = mg_acc[...].astype(BF16)
    part_mid[:, :, n_o:n_om] = mix_low.reshape(n_cores, block, 128)
    sum_send(ids.sum_mid, part_mid, got_mid, lat_mix)

    for e in range(n_e):
        arrive(ids.core_sib + e, core_s.at[:, :, e])
    rs_step(1, *core_args, ids.core_z)

    lax.fori_loop(0, n_e, backward, 0)
    part_mid[:, :, pg_cols] = pg_acc[...].astype(BF16).reshape(n_cores, block, n_i)
    sum_send(ids.sum_mid + n_peers, part_mid, got_mid, pg_cols)

    expert_full = dot_tn(gate_low, mix_low) * inv_rows
    pick = (
        lax.broadcasted_iota(jnp.int32, (128, 128), 0)
        == lax.broadcasted_iota(jnp.int32, (128, 128), 1) + c * n_e
    ).astype(BF16)
    expert_term = dot_nn(expert_full.astype(BF16), pick)

    for k in range(n_peers):
        arrive(ids.factor + k, ef_all.at[behind[k]])
    total = sum_wait(ids.sum_mid, part_mid, got_mid, lat_mix)
    mix_block = total[:, n_o : n_o + n_cores * n_e].astype(BF16)
    gate_grad = dot_nn(mix_block, ef_all[...].reshape(n_cores * n_e, n_g).astype(BF16))
    gate = gates[...]
    n_og = n_o + n_g
    lat_logit = slice(0, n_og)
    pg_held = slice(n_og, n_og + n_i)
    held_mid[c, :, :n_o] = total[:, :n_o].astype(BF16)
    held_mid[c, :, n_o:n_og] = (gate_grad * gate * (1.0 - gate)).astype(BF16)
    share_send(ids.share_mid, held_mid, lat_logit)

    rs_step(2, *core_args, ids.core_z)

    held_mid[c, :, pg_held] = sum_wait(
        ids.sum_mid + n_peers, part_mid, got_mid, pg_cols
    ).astype(BF16)
    share_send(ids.share_mid + n_peers, held_mid, pg_held)

    share_wait(ids.share_mid, held_mid, lat_logit)
    latent = held_mid[:, :, :n_o].reshape(rows, n_o)
    logit_grad = held_mid[:, :, n_o:n_og].reshape(rows, n_g)
    blk = (2, n_z, 2)
    g_rows = n_g // n_dp
    fac_b[:, :, :, :i_rows] = (
        (dot_tn(latent, og[...]) * inv_rows).astype(BF16).reshape(*blk, i_rows, width)
    )
    router_term = (dot_tn(logit_grad, tok[...]) * inv_rows).reshape(*blk, g_rows, width)
    expert_wide = jnp.concatenate(
        [expert_term, jnp.zeros((n_g, width - 128), F32)], axis=1
    ) if width > 128 else expert_term
    fac_b[:, :, :, i_rows:] = jnp.concatenate(
        [router_term, expert_wide.reshape(*blk, g_rows, width)], axis=3
    ).astype(BF16)
    send(ids.out_sib, fac_b.at[:, :, 1 - core], fac_s, sib)

    rs_step(3, *core_args, ids.core_z)

    arrive(ids.out_sib, fac_s)
    rs_step(1, *fac_o, ids.out_z)

    share_wait(ids.share_mid + n_peers, held_mid, pg_held)
    pgrad = held_mid[:, :, pg_held].reshape(rows, n_i)
    inp_b[...] = (dot_tn(pgrad, tok[...]) * inv_rows).astype(BF16).reshape(*blk, i_rows, width)
    send(ids.inp_sib, inp_b.at[:, :, 1 - core], inp_s, sib)

    for s in range(4, steps + 1):
        rs_step(s, *core_args, ids.core_z)
    arrive(ids.inp_sib, inp_s)
    rs_step(1, *fac_i, ids.inp_z)
    rs_step(2, *fac_o, ids.out_z)

    mixed_v[...] = dot_nn(latent, outf[...]).astype(BF16)
    results = [pltpu.make_async_copy(mixed_v, mixed_ref, out_sem.at[0])]
    results[0].start()

    rs_turn(*core_args, core_yr, ids.core_z, ids.core_y)
    rs_step(2, *fac_i, ids.inp_z)
    rs_step(3, *fac_o, ids.out_z)
    tgrad_v[...] = (dot_nn(pgrad, inf[...]) + dot_nn(logit_grad, rw[...])).astype(BF16)

    def result(src, dst):
        results.append(pltpu.make_async_copy(src, dst, out_sem.at[len(results)]))
        results[-1].start()

    result(tgrad_v, tgrad_ref)
    rs_step(3, *fac_i, ids.inp_z)
    for s in range(4, steps + 1):
        rs_step(s, *fac_o, ids.out_z)
        rs_step(s, *fac_i, ids.inp_z)
    rs_turn(*fac_o, fac_yr, ids.out_z, ids.out_y)
    rs_turn(*fac_i, inp_yr, ids.inp_z, ids.inp_y)
    cgrad_v[...] = jnp.swapaxes(rs_end(*core_args, core_yr, ids.core_z, ids.core_y), 0, 1)
    result(cgrad_v, cgrad_ref)
    val = rs_end(*fac_o, fac_yr, ids.out_z, ids.out_y)
    ograd_v[...] = val[:i_rows]
    rgrad_v[...] = val[i_rows : i_rows + g_rows]
    egrad_v[...] = val[i_rows + g_rows :, :n_e]
    result(ograd_v, ograd_ref)
    result(rgrad_v, rgrad_ref)
    result(egrad_v, egrad_ref)
    igrad_v[...] = rs_end(*fac_i, inp_yr, ids.inp_z, ids.inp_y)
    result(igrad_v, igrad_ref)

    for d in sent:
        d.wait_send()

    def drain(e, _):
        core_sib(e).wait_send()
        return 0

    lax.fori_loop(0, n_e, drain, 0)
    for r in results:
        r.wait()


def hand_over(n, *refs):
    srcs, dsts, held = refs[:n], refs[n : 2 * n], refs[2 * n : 3 * n]
    in_sem, out_sem = refs[3 * n :]
    ins = [pltpu.make_async_copy(srcs[i], held[i], in_sem.at[i]) for i in range(n)]
    outs = [pltpu.make_async_copy(held[i], dsts[i], out_sem.at[i]) for i in range(n)]
    for copy in ins:
        copy.start()
    for i in range(n):
        ins[i].wait()
        outs[i].start()
    for copy in outs:
        copy.wait()


def peers_from(y_hi, x, n_x):
    out = []
    for dy in range(2):
        for dx in range(n_x):
            if dy or dx:
                out.append(lax.rem(y_hi + dy, 2) * n_x + lax.rem(x + n_x - dx, n_x))
    return out


def shards(n_dp, n_cores, tokens, router_weight, expert_factor, input_factor, core_tensor,
           output_factor, out_grad):
    n_z = n_dp // 4
    steps = n_z // 2
    rows, width = tokens.shape
    n_g = router_weight.shape[0]
    n_i = input_factor.shape[0]
    n_o = output_factor.shape[0]
    i_rows, n_e, _ = core_tensor.shape
    g_rows = n_g // n_dp
    block = rows // n_cores
    cblk = (n_e, i_rows, n_o)
    fblk = (i_rows + 2 * g_rows, width)
    iblk = (i_rows, width)
    in_cols = n_g + n_i + n_o
    mid_cols = n_o + n_i + 128
    ids = Ids(n_z, n_cores, n_e)
    sds = jax.ShapeDtypeStruct
    results = (
        sds((rows, width), BF16),
        sds((rows, width), BF16),
        sds((i_rows, n_e, n_o), F32),
        sds((i_rows, width), F32),
        sds((g_rows, width), F32),
        sds((i_rows, width), F32),
        sds((g_rows, n_e), F32),
    )
    vmem = pltpu.VMEM
    scratch = [vmem(r.shape, r.dtype) for r in results] + [
        vmem((rows, width), BF16),
        vmem((n_g, width), BF16),
        vmem((n_e, n_g), BF16),
        vmem((n_i, width), BF16),
        vmem((n_o, width), BF16),
        vmem((rows, width), BF16),
        vmem((i_rows, n_e, n_o), BF16),
        vmem((2, n_z, 2) + cblk, BF16),
        vmem((n_cores, n_e, n_g), F32),
        vmem((n_cores, block, in_cols), F32),
        vmem((n_cores - 1, block, in_cols), F32),
        vmem((n_cores, block, in_cols), BF16),
        vmem((block, n_g), F32),
        vmem((n_cores, block, mid_cols), BF16),
        vmem((n_cores - 1, block, mid_cols), BF16),
        vmem((n_cores, block, in_cols), BF16),
        vmem((n_e, rows, 128), F32),
        vmem((n_e, rows, n_o), BF16),
        vmem((rows, n_o), F32),
        vmem((rows, n_i), F32),
        vmem((rows, 128), F32),
        vmem((2, n_z, 2) + cblk, BF16),
        vmem((2, n_z) + cblk, BF16),
        vmem((2, 2, steps) + cblk, BF16),
        vmem(cblk, BF16),
        vmem((2, n_z, 2) + fblk, BF16),
        vmem((2, n_z) + fblk, BF16),
        vmem((2, 2, steps) + fblk, BF16),
        vmem(fblk, BF16),
        vmem((2, n_z, 2) + iblk, BF16),
        vmem((2, n_z) + iblk, BF16),
        vmem((2, 2, steps) + iblk, BF16),
        vmem(iblk, BF16),
        pltpu.SemaphoreType.DMA((7,)),
        pltpu.SemaphoreType.DMA((7,)),
        pltpu.SemaphoreType.DMA((ids.count,)),
        pltpu.SemaphoreType.DMA((ids.count,)),
    ]
    outs = pl.pallas_call(
        functools.partial(kernel, n_z, n_cores),
        out_shape=results,
        in_specs=[pl.BlockSpec(memory_space=pl.ANY)] * 7,
        out_specs=[pl.BlockSpec(memory_space=pl.ANY)] * 7,
        scratch_shapes=scratch,
        compiler_params=pltpu.CompilerParams(
            collective_id=0, has_side_effects=True, vmem_limit_bytes=56 * 1024 * 1024
        ),
    )(tokens, router_weight, expert_factor.T, input_factor, core_tensor, output_factor, out_grad)
    return pl.pallas_call(
        functools.partial(hand_over, len(results)),
        out_shape=results,
        in_specs=[pl.BlockSpec(memory_space=pl.ANY)] * 7,
        out_specs=[pl.BlockSpec(memory_space=pl.ANY)] * 7,
        scratch_shapes=[vmem(r.shape, r.dtype) for r in results]
        + [pltpu.SemaphoreType.DMA((7,))] * 2,
    )(*outs)


def solution(mesh):
    return jax.shard_map(
        functools.partial(shards, mesh.shape["dp"], mesh.shape["cores"]),
        mesh=mesh,
        in_specs=(
            P("dp", "cores"),
            P(None, "cores"),
            P(None, "cores"),
            P(None, "cores"),
            P("dp", "cores", None),
            P(None, "cores"),
            P("dp", "cores"),
        ),
        out_specs=(
            P("dp", "cores"),
            P("dp", "cores"),
            P("dp", "cores", None),
            P("dp", "cores"),
            P("dp", "cores"),
            P("dp", "cores"),
            P("dp", "cores"),
        ),
        check_vma=False,
    )
```

```python
import functools

import jax
import jax.numpy as jnp
from jax import lax
from jax.experimental import pallas as pl
from jax.experimental.pallas import tpu as pltpu
from jax.sharding import PartitionSpec as P

MESH = pl.DeviceIdType.MESH
F32 = jnp.float32
BF16 = jnp.bfloat16


def dot_nn(a, b):
    return lax.dot_general(a, b, (((1,), (0,)), ((), ())), preferred_element_type=F32)


def dot_nt(a, b):
    return lax.dot_general(a, b, (((1,), (1,)), ((), ())), preferred_element_type=F32)


def dot_tn(a, b):
    return lax.dot_general(a, b, (((0,), (0,)), ((), ())), preferred_element_type=F32)


def ring_hops(n_z):
    up = n_z // 2
    down = n_z - 1 - up
    return ((up, down), (down, up))


class Ids:
    def __init__(self, n_z, n_cores, n_e):
        self.count = 0
        steps = n_z // 2
        self.gather_y = self.take(1)
        self.gather_z = self.take(4 * steps)
        self.gather_sib = self.take(2 * n_z)
        self.factor = self.take(n_cores - 1)
        self.sum_in = self.take(2 * (n_cores - 1))
        self.share_in = self.take(2 * (n_cores - 1))
        self.sum_mid = self.take(2 * (n_cores - 1))
        self.share_mid = self.take(2 * (n_cores - 1))
        self.core_sib = self.take(2)
        self.core_z = self.take(4 * steps)
        self.core_y = self.take(1)
        self.out_sib = self.take(1)
        self.out_z = self.take(4 * steps)
        self.out_y = self.take(1)
        self.inp_sib = self.take(1)
        self.inp_z = self.take(4 * steps)
        self.inp_y = self.take(1)

    def take(self, n):
        first = self.count
        self.count += n
        return first


def kernel(
    n_z, n_cores,
    tok_hbm, rw_hbm, ef_hbm, inf_hbm, core_hbm, outf_hbm, og_hbm,
    mixed_ref, tgrad_ref, cgrad_ref, igrad_ref, rgrad_ref, ograd_ref, egrad_ref,
    mixed_v, tgrad_v, cgrad_v, igrad_v, rgrad_v, ograd_v, egrad_v,
    tok, rw, ef, inf, outf, og, core_v,
    whole, ef_all, part_a, got_a, held_a, part_p, got_p, held_p, gates, part_mid, got_mid, held_mid,
    mix_b, sib_a, sib_mix, proj_t, sib_pt, lat_acc, pg_acc, mg_acc,
    core_b, core_r, core_yr,
    fac_b, fac_s, fac_r, fac_yr,
    inp_b, inp_s, inp_r, inp_yr,
    in_sem, out_sem, ss, rs,
):
    rows, width = tok.shape
    n_g = rw.shape[0]
    n_i = inf.shape[0]
    n_o = outf.shape[0]
    n_e = ef.shape[0]
    block = rows // n_cores
    i_rows = whole.shape[4]
    n_dp = 4 * n_z
    inv_rows = 1.0 / rows
    ids = Ids(n_z, n_cores, n_e)
    steps = n_z // 2
    hops = ring_hops(n_z)

    dp = lax.axis_index("dp")
    c = lax.axis_index("cores")
    core = lax.rem(dp, 2)
    z = lax.rem(dp // 2, n_z)
    y = dp // (2 * n_z)

    def at(yy, zz, kk):
        return ((yy * n_z + zz) * 2 + kk, c)

    def zmod(offset):
        return lax.rem(z + offset + 2 * n_z, n_z)

    sib = at(y, z, 1 - core)
    ynb = at(1 - y, z, core)
    znb = (at(y, zmod(1), core), at(y, zmod(-1), core))
    n_x = n_cores // 2
    y_hi = c // n_x
    x = lax.rem(c, n_x)
    peers = []
    for dy in range(2):
        for dx in range(n_x):
            if dy or dx:
                other = lax.rem(y_hi + dy, 2) * n_x + lax.rem(x + dx, n_x)
                peers.append((dp, other))

    sent = []

    def send(i, src, dst, dev):
        d = pltpu.make_async_remote_copy(
            src, dst, ss.at[i], rs.at[i], device_id=dev, device_id_type=MESH
        )
        d.start()
        sent.append(d)

    def arrive(i, ref):
        pltpu.make_async_remote_copy(
            ref, ref, ss.at[i], rs.at[i], device_id=sib, device_id_type=MESH
        ).wait_recv()

    loads = [
        pltpu.make_async_copy(src, dst, in_sem.at[n])
        for n, (src, dst) in enumerate(
            (
                (core_hbm, core_v),
                (og_hbm, og),
                (outf_hbm, outf),
                (tok_hbm, tok),
                (rw_hbm, rw),
                (inf_hbm, inf),
                (ef_hbm, ef),
            )
        )
    ]
    for load in loads:
        load.start()

    barrier = pltpu.get_barrier_semaphore()
    greet = [sib, ynb, znb[0], znb[1]] + peers
    for dev in greet:
        pl.semaphore_signal(barrier, inc=1, device_id=dev, device_id_type=MESH)
    loads[0].wait()
    whole[y, z, core] = jnp.swapaxes(core_v[...].astype(F32), 0, 1).astype(BF16)
    pl.semaphore_wait(barrier, len(greet))

    lane_y = (y, 1 - y)

    def ag_id(lane, way, s):
        return ids.gather_z + (lane * 2 + way) * steps + s - 1

    def ag_ref(lane, zz):
        return whole.at[lane_y[lane], zz, core]

    def ag_sib(lane, offset):
        ref = ag_ref(lane, zmod(offset))
        send(ids.gather_sib + lane * n_z + offset % n_z, ref, ref, sib)

    def ag_open(lane):
        ref = ag_ref(lane, z)
        for way in range(2):
            if hops[lane][way] >= 1:
                send(ag_id(lane, way, 1), ref, ref, znb[way])
        ag_sib(lane, 0)

    def ag_step(s, lane):
        for way in range(2):
            if s <= hops[lane][way]:
                offset = -s if way == 0 else s
                ref = ag_ref(lane, zmod(offset))
                arrive(ag_id(lane, way, s), ref)
                if s + 1 <= hops[lane][way]:
                    send(ag_id(lane, way, s + 1), ref, ref, znb[way])
                ag_sib(lane, offset)

    def ag_close():
        for lane in range(2):
            for offset in range(n_z):
                ref = whole.at[lane_y[lane], zmod(offset), 1 - core]
                arrive(ids.gather_sib + lane * n_z + offset, ref)

    behind = peers_from(y_hi, x, n_x)
    n_peers = n_cores - 1

    def sum_send(first, src, got, cols):
        for k, dev in enumerate(peers):
            send(first + k, src.at[dev[1], :, cols], got.at[k, :, cols], dev)

    def sum_wait(first, src, got, cols):
        for k in range(n_peers):
            arrive(first + k, got.at[k, :, cols])
        total = src[c, :, cols].astype(F32)
        for k in range(n_peers):
            total = total + got[k, :, cols].astype(F32)
        return total

    def share_send(first, held, cols):
        for k, dev in enumerate(peers):
            send(first + k, held.at[c, :, cols], held.at[c, :, cols], dev)

    def share_wait(first, held, cols):
        for k in range(n_peers):
            arrive(first + k, held.at[behind[k], :, cols])

    send(ids.gather_y, ag_ref(0, z), ag_ref(0, z), ynb)
    ag_open(0)

    n_go = n_g + n_o
    everything = slice(None)
    loads[1].wait()
    loads[2].wait()
    part_a[:, :, n_g:] = dot_nt(og[...], outf[...]).astype(BF16).reshape(n_cores, block, n_o)
    loads[3].wait()
    loads[4].wait()
    part_a[:, :, :n_g] = dot_nt(tok[...], rw[...]).astype(BF16).reshape(n_cores, block, n_g)
    sum_send(ids.sum_in, part_a, got_a, everything)
    loads[5].wait()
    part_p[...] = dot_nt(tok[...], inf[...]).reshape(n_cores, block, n_i)
    sum_send(ids.sum_in + n_peers, part_p, got_p, everything)
    loads[6].wait()
    ef_all[c] = ef[...].astype(F32)
    for k, dev in enumerate(peers):
        send(ids.factor + k, ef_all.at[c], ef_all.at[c], dev)

    arrive(ids.gather_y, ag_ref(1, z))
    ag_open(1)
    ag_step(1, 0)
    ag_step(1, 1)

    total = sum_wait(ids.sum_in, part_a, got_a, everything)
    gate = jax.nn.sigmoid(total[:, :n_g])
    gates[...] = gate
    held_a[c, :, :n_g] = gate.astype(BF16)
    held_a[c, :, n_g:] = total[:, n_g:].astype(BF16)
    share_send(ids.share_in, held_a, everything)

    ag_step(2, 0)

    held_p[c] = sum_wait(ids.sum_in + n_peers, part_p, got_p, everything).astype(BF16)
    share_send(ids.share_in + n_peers, held_p, everything)

    ag_step(2, 1)
    ag_step(3, 0)

    def wide(v, n):
        return jnp.concatenate([v] * (n // 128), axis=1)

    def spread_mixing(held, out):
        mixing = dot_nt(held[:, :, :n_g].reshape(rows, n_g), ef[...])
        for e in range(n_e):
            out[e] = jnp.broadcast_to(mixing[:, e : e + 1], (rows, 128))

    share_wait(ids.share_in, held_a, everything)
    send(ids.core_sib, held_a, sib_a, sib)
    spread_mixing(held_a, mix_b)
    lgrad = held_a[:, :, n_g:].reshape(rows, n_o)
    lgrad_wide = lgrad.astype(F32)

    ag_step(3, 1)

    share_wait(ids.share_in + n_peers, held_p, everything)
    proj = held_p[...].reshape(rows, n_i)
    proj_t[...] = proj.T.reshape(2 * n_z, 2, i_rows, rows)
    send(ids.core_sib + 1, proj_t.at[:, 1 - core], sib_pt, sib)
    arrive(ids.core_sib, sib_a)
    spread_mixing(sib_a, sib_mix)
    sib_lgrad = sib_a[:, :, n_g:].reshape(rows, n_o).astype(F32)
    half = 2 * n_z * i_rows
    own_t = proj_t[:, core].reshape(half, rows)
    arrive(ids.core_sib + 1, sib_pt)
    sib_t = sib_pt[...].reshape(half, rows)

    def core_terms(e, _):
        own = (wide(mix_b[e], n_o) * lgrad_wide).astype(BF16)
        other = (wide(sib_mix[e], n_o) * sib_lgrad).astype(BF16)
        term = (dot_nn(own_t, own) + dot_nn(sib_t, other)) * inv_rows
        core_b[:, :, e] = term.astype(BF16).reshape(2, n_z, i_rows, n_o)
        return 0

    lax.fori_loop(0, n_e, core_terms, 0)

    def rs_ring(block_of, sib_of, got, yr, z_id, y_id):
        def num(lane, way, s):
            return z_id + (lane * 2 + way) * steps + s - 1

        def base(lane, d):
            val = block_of(lane_y[lane], d)[...].astype(F32)
            if sib_of is not None:
                val = val + sib_of(lane_y[lane], d)[...].astype(F32)
            return val

        def step(s):
            for lane in range(2):
                for way in range(2):
                    k = hops[lane][way]
                    if s <= k:
                        far = k - s + 1
                        d = zmod(far if way == 0 else -far)
                        out = block_of(lane_y[lane], d)
                        if s > 1:
                            arrive(num(lane, way, s - 1), got.at[lane, way, s - 2])
                            val = base(lane, d) + got[lane, way, s - 2].astype(F32)
                            out[...] = val.astype(BF16)
                        elif sib_of is not None:
                            out[...] = base(lane, d).astype(BF16)
                        send(num(lane, way, s), out, got.at[lane, way, s - 1], znb[way])

        def lane_sum(lane):
            val = base(lane, z)
            for way in range(2):
                k = hops[lane][way]
                if k:
                    arrive(num(lane, way, k), got.at[lane, way, k - 1])
                    val = val + got[lane, way, k - 1].astype(F32)
            return val

        def turn():
            val = lane_sum(1)
            out = block_of(1 - y, z)
            out[...] = val.astype(BF16)
            send(y_id, out, yr, ynb)

        def end():
            val = lane_sum(0)
            arrive(y_id, yr)
            return val + yr[...].astype(F32)

        return step, turn, end

    core_step, core_turn, core_end = rs_ring(
        lambda yy, d: core_b.at[yy, d], None, core_r, core_yr, ids.core_z, ids.core_y
    )
    out_step, out_turn, out_end = rs_ring(
        lambda yy, d: fac_b.at[yy, d, core],
        lambda yy, d: fac_s.at[yy, d],
        fac_r, fac_yr, ids.out_z, ids.out_y,
    )
    inp_step, inp_turn, inp_end = rs_ring(
        lambda yy, d: inp_b.at[yy, d, core],
        lambda yy, d: inp_s.at[yy, d],
        inp_r, inp_yr, ids.inp_z, ids.inp_y,
    )

    core_step(1)
    for s in range(4, steps + 1):
        ag_step(s, 0)
        ag_step(s, 1)
    ag_close()

    lat_acc[...] = jnp.zeros_like(lat_acc)
    pg_acc[...] = jnp.zeros_like(pg_acc)
    mg_acc[...] = jnp.zeros_like(mg_acc)
    lane_no = lax.broadcasted_iota(jnp.int32, (rows, 128), 1)

    def forward(e, _):
        expanded = dot_nn(proj, whole[:, :, :, e].reshape(n_i, n_o))
        lat_acc[...] += wide(mix_b[e], n_o) * expanded
        col = jnp.sum(lgrad_wide * expanded, axis=1, keepdims=True)
        mg_acc[...] += jnp.where(lane_no == c * n_e + e, col, 0.0)
        return 0

    def backward(e, _):
        spread = dot_nt(lgrad, whole[:, :, :, e].reshape(n_i, n_o))
        pg_acc[...] += wide(mix_b[e], n_i) * spread
        return 0

    n_om = n_o + 128
    lat_mix = slice(0, n_om)
    pg_cols = slice(n_om, n_om + n_i)
    lax.fori_loop(0, n_e, forward, 0)
    part_mid[:, :, :n_o] = lat_acc[...].astype(BF16).reshape(n_cores, block, n_o)
    mix_low = mg_acc[...].astype(BF16)
    part_mid[:, :, n_o:n_om] = mix_low.reshape(n_cores, block, 128)
    sum_send(ids.sum_mid, part_mid, got_mid, lat_mix)


    lax.fori_loop(0, n_e, backward, 0)
    part_mid[:, :, pg_cols] = pg_acc[...].astype(BF16).reshape(n_cores, block, n_i)
    sum_send(ids.sum_mid + n_peers, part_mid, got_mid, pg_cols)

    gate_low = held_a[:, :, :n_g].reshape(rows, n_g)
    expert_full = dot_tn(gate_low, mix_low) * inv_rows
    pick = (
        lax.broadcasted_iota(jnp.int32, (128, 128), 0)
        == lax.broadcasted_iota(jnp.int32, (128, 128), 1) + c * n_e
    ).astype(BF16)
    expert_term = dot_nn(expert_full.astype(BF16), pick)
    core_step(2)

    for k in range(n_peers):
        arrive(ids.factor + k, ef_all.at[behind[k]])
    total = sum_wait(ids.sum_mid, part_mid, got_mid, lat_mix)
    mix_block = total[:, n_o : n_o + n_cores * n_e].astype(BF16)
    gate_grad = dot_nn(mix_block, ef_all[...].reshape(n_cores * n_e, n_g).astype(BF16))
    gate = gates[...]
    n_og = n_o + n_g
    lat_logit = slice(0, n_og)
    pg_held = slice(n_og, n_og + n_i)
    held_mid[c, :, :n_o] = total[:, :n_o].astype(BF16)
    held_mid[c, :, n_o:n_og] = (gate_grad * gate * (1.0 - gate)).astype(BF16)
    share_send(ids.share_mid, held_mid, lat_logit)

    core_step(3)

    held_mid[c, :, pg_held] = sum_wait(
        ids.sum_mid + n_peers, part_mid, got_mid, pg_cols
    ).astype(BF16)
    share_send(ids.share_mid + n_peers, held_mid, pg_held)

    share_wait(ids.share_mid, held_mid, lat_logit)
    latent = held_mid[:, :, :n_o].reshape(rows, n_o)
    logit_grad = held_mid[:, :, n_o:n_og].reshape(rows, n_g)
    blk = (2, n_z, 2)
    g_rows = n_g // n_dp
    mid = width // 2
    w_router = width + mid
    fac_b[:, :, :, :, :width] = (
        (dot_tn(latent, og[...]) * inv_rows).astype(BF16).reshape(*blk, i_rows, width)
    )
    router_term = (dot_tn(logit_grad, tok[...]) * inv_rows).reshape(*blk, g_rows, width)
    fac_b[:, :, :, :, width:w_router] = jnp.concatenate(
        [router_term[..., :mid], router_term[..., mid:]], axis=3
    ).astype(BF16)
    expert_blocks = expert_term.reshape(*blk, g_rows, 128)
    fac_b[:, :, :, :, w_router:] = jnp.concatenate(
        [expert_blocks, jnp.zeros_like(expert_blocks)], axis=3
    ).astype(BF16)
    send(ids.out_sib, fac_b.at[:, :, 1 - core], fac_s, sib)

    for s in range(4, steps + 1):
        core_step(s)

    arrive(ids.out_sib, fac_s)
    out_step(1)

    share_wait(ids.share_mid + n_peers, held_mid, pg_held)
    pgrad = held_mid[:, :, pg_held].reshape(rows, n_i)
    inp_b[...] = (dot_tn(pgrad, tok[...]) * inv_rows).astype(BF16).reshape(*blk, i_rows, width)
    send(ids.inp_sib, inp_b.at[:, :, 1 - core], inp_s, sib)

    out_step(2)
    arrive(ids.inp_sib, inp_s)
    inp_step(1)

    mixed_v[...] = dot_nn(latent, outf[...]).astype(BF16)
    results = []

    def result(src, dst):
        results.append(pltpu.make_async_copy(src, dst, out_sem.at[len(results)]))
        results[-1].start()

    result(mixed_v, mixed_ref)
    core_turn()
    out_step(3)
    inp_step(2)
    tgrad_v[...] = (dot_nn(pgrad, inf[...]) + dot_nn(logit_grad, rw[...])).astype(BF16)
    result(tgrad_v, tgrad_ref)
    for s in range(4, steps + 1):
        out_step(s)
        inp_step(s - 1)
    out_turn()
    if steps >= 4:
        inp_step(steps)
    cgrad_v[...] = jnp.swapaxes(core_end(), 0, 1)
    result(cgrad_v, cgrad_ref)
    inp_turn()
    val = out_end()
    ograd_v[...] = val[:, :width]
    rgrad_v[:, :mid] = val[:g_rows, width:w_router]
    rgrad_v[:, mid:] = val[g_rows:, width:w_router]
    egrad_v[...] = val[:g_rows, w_router : w_router + n_e]
    result(ograd_v, ograd_ref)
    result(rgrad_v, rgrad_ref)
    result(egrad_v, egrad_ref)
    igrad_v[...] = inp_end()
    result(igrad_v, igrad_ref)

    for d in sent:
        d.wait_send()
    for r in results:
        r.wait()


def hand_over(n, *refs):
    srcs, dsts, held = refs[:n], refs[n : 2 * n], refs[2 * n : 3 * n]
    in_sem, out_sem = refs[3 * n :]
    ins = [pltpu.make_async_copy(srcs[i], held[i], in_sem.at[i]) for i in range(n)]
    outs = [pltpu.make_async_copy(held[i], dsts[i], out_sem.at[i]) for i in range(n)]
    for copy in ins:
        copy.start()
    for i in range(n):
        ins[i].wait()
        outs[i].start()
    for copy in outs:
        copy.wait()


def peers_from(y_hi, x, n_x):
    out = []
    for dy in range(2):
        for dx in range(n_x):
            if dy or dx:
                out.append(lax.rem(y_hi + dy, 2) * n_x + lax.rem(x + n_x - dx, n_x))
    return out


def shards(n_dp, n_cores, tokens, router_weight, expert_factor, input_factor, core_tensor,
           output_factor, out_grad):
    n_z = n_dp // 4
    steps = n_z // 2
    rows, width = tokens.shape
    n_g = router_weight.shape[0]
    n_i = input_factor.shape[0]
    n_o = output_factor.shape[0]
    i_rows, n_e, _ = core_tensor.shape
    g_rows = n_g // n_dp
    block = rows // n_cores
    cblk = (n_e, i_rows, n_o)
    fblk = (i_rows, width + width // 2 + 128)
    iblk = (i_rows, width)
    in_cols = n_g + n_i + n_o
    mid_cols = n_o + n_i + 128
    ids = Ids(n_z, n_cores, n_e)
    sds = jax.ShapeDtypeStruct
    results = (
        sds((rows, width), BF16),
        sds((rows, width), BF16),
        sds((i_rows, n_e, n_o), F32),
        sds((i_rows, width), F32),
        sds((g_rows, width), F32),
        sds((i_rows, width), F32),
        sds((g_rows, n_e), F32),
    )
    vmem = pltpu.VMEM
    scratch = [vmem(r.shape, r.dtype) for r in results] + [
        vmem((rows, width), BF16),
        vmem((n_g, width), BF16),
        vmem((n_e, n_g), BF16),
        vmem((n_i, width), BF16),
        vmem((n_o, width), BF16),
        vmem((rows, width), BF16),
        vmem((i_rows, n_e, n_o), BF16),
        vmem((2, n_z, 2) + cblk, BF16),
        vmem((n_cores, n_e, n_g), F32),
        vmem((n_cores, block, n_g + n_o), BF16),
        vmem((n_cores - 1, block, n_g + n_o), BF16),
        vmem((n_cores, block, n_g + n_o), BF16),
        vmem((n_cores, block, n_i), F32),
        vmem((n_cores - 1, block, n_i), F32),
        vmem((n_cores, block, n_i), BF16),
        vmem((block, n_g), F32),
        vmem((n_cores, block, mid_cols), BF16),
        vmem((n_cores - 1, block, mid_cols), BF16),
        vmem((n_cores, block, in_cols), BF16),
        vmem((n_e, rows, 128), F32),
        vmem((n_cores, block, n_g + n_o), BF16),
        vmem((n_e, rows, 128), F32),
        vmem((2 * n_z, 2, i_rows, rows), BF16),
        vmem((2 * n_z, i_rows, rows), BF16),
        vmem((rows, n_o), F32),
        vmem((rows, n_i), F32),
        vmem((rows, 128), F32),
        vmem((2, n_z) + cblk, BF16),
        vmem((2, 2, steps) + cblk, BF16),
        vmem(cblk, BF16),
        vmem((2, n_z, 2) + fblk, BF16),
        vmem((2, n_z) + fblk, BF16),
        vmem((2, 2, steps) + fblk, BF16),
        vmem(fblk, BF16),
        vmem((2, n_z, 2) + iblk, BF16),
        vmem((2, n_z) + iblk, BF16),
        vmem((2, 2, steps) + iblk, BF16),
        vmem(iblk, BF16),
        pltpu.SemaphoreType.DMA((7,)),
        pltpu.SemaphoreType.DMA((7,)),
        pltpu.SemaphoreType.DMA((ids.count,)),
        pltpu.SemaphoreType.DMA((ids.count,)),
    ]
    outs = pl.pallas_call(
        functools.partial(kernel, n_z, n_cores),
        out_shape=results,
        in_specs=[pl.BlockSpec(memory_space=pl.ANY)] * 7,
        out_specs=[pl.BlockSpec(memory_space=pl.ANY)] * 7,
        scratch_shapes=scratch,
        compiler_params=pltpu.CompilerParams(
            collective_id=0, has_side_effects=True, vmem_limit_bytes=56 * 1024 * 1024
        ),
    )(tokens, router_weight, expert_factor.T, input_factor, core_tensor, output_factor, out_grad)
    return pl.pallas_call(
        functools.partial(hand_over, len(results)),
        out_shape=results,
        in_specs=[pl.BlockSpec(memory_space=pl.ANY)] * 7,
        out_specs=[pl.BlockSpec(memory_space=pl.ANY)] * 7,
        scratch_shapes=[vmem(r.shape, r.dtype) for r in results]
        + [pltpu.SemaphoreType.DMA((7,))] * 2,
    )(*outs)


def solution(mesh):
    return jax.shard_map(
        functools.partial(shards, mesh.shape["dp"], mesh.shape["cores"]),
        mesh=mesh,
        in_specs=(
            P("dp", "cores"),
            P(None, "cores"),
            P(None, "cores"),
            P(None, "cores"),
            P("dp", "cores", None),
            P(None, "cores"),
            P("dp", "cores"),
        ),
        out_specs=(
            P("dp", "cores"),
            P("dp", "cores"),
            P("dp", "cores", None),
            P("dp", "cores"),
            P("dp", "cores"),
            P("dp", "cores"),
            P("dp", "cores"),
        ),
        check_vma=False,
    )
```

```python
import functools

import jax
import jax.numpy as jnp
from jax import lax
from jax.experimental import pallas as pl
from jax.experimental.pallas import tpu as pltpu
from jax.sharding import PartitionSpec as P

MESH = pl.DeviceIdType.MESH
F32 = jnp.float32
BF16 = jnp.bfloat16


def dot_nn(a, b):
    return lax.dot_general(a, b, (((1,), (0,)), ((), ())), preferred_element_type=F32)


def dot_nt(a, b):
    return lax.dot_general(a, b, (((1,), (1,)), ((), ())), preferred_element_type=F32)


def dot_tn(a, b):
    return lax.dot_general(a, b, (((0,), (0,)), ((), ())), preferred_element_type=F32)


def ring_hops(n_z):
    up = n_z // 2
    down = n_z - 1 - up
    return ((up, down), (down, up))


class Ids:
    def __init__(self, n_z, n_cores, n_e):
        self.count = 0
        steps = n_z // 2
        self.gather_y = self.take(1)
        self.gather_z = self.take(4 * steps)
        self.gather_sib = self.take(2 * n_z)
        self.factor = self.take(n_cores - 1)
        self.sum_in = self.take(2 * (n_cores - 1))
        self.share_in = self.take(2 * (n_cores - 1))
        self.sum_mid = self.take(2 * (n_cores - 1))
        self.share_mid = self.take(2 * (n_cores - 1))
        self.core_sib = self.take(2)
        self.core_z = self.take(4 * steps)
        self.core_y = self.take(1)
        self.out_sib = self.take(1)
        self.out_z = self.take(4 * steps)
        self.out_y = self.take(1)
        self.inp_sib = self.take(1)
        self.inp_z = self.take(4 * steps)
        self.inp_y = self.take(1)

    def take(self, n):
        first = self.count
        self.count += n
        return first


def kernel(
    n_z, n_cores,
    tok_hbm, rw_hbm, ef_hbm, inf_hbm, core_hbm, outf_hbm, og_hbm,
    mixed_ref, tgrad_ref, cgrad_ref, igrad_ref, rgrad_ref, ograd_ref, egrad_ref,
    mixed_v, tgrad_v, cgrad_v, igrad_v, rgrad_v, ograd_v, egrad_v,
    tok, rw, ef, inf, outf, og, core_v,
    whole, ef_all, part_a, got_a, held_a, part_p, got_p, held_p, gates, part_mid, got_mid, held_mid,
    mix_b, sib_a, sib_mix, proj_t, sib_pt, lat_acc, pg_acc, mg_acc,
    core_b, core_r, core_yr,
    fac_b, fac_s, fac_r, fac_yr,
    inp_b, inp_s, inp_r, inp_yr,
    in_sem, out_sem, ss, rs,
):
    rows, width = tok.shape
    n_g = rw.shape[0]
    n_i = inf.shape[0]
    n_o = outf.shape[0]
    n_e = ef.shape[0]
    block = rows // n_cores
    i_rows = whole.shape[4]
    n_dp = 4 * n_z
    inv_rows = 1.0 / rows
    ids = Ids(n_z, n_cores, n_e)
    steps = n_z // 2
    hops = ring_hops(n_z)

    dp = lax.axis_index("dp")
    c = lax.axis_index("cores")
    core = lax.rem(dp, 2)
    z = lax.rem(dp // 2, n_z)
    y = dp // (2 * n_z)

    def at(yy, zz, kk):
        return ((yy * n_z + zz) * 2 + kk, c)

    def zmod(offset):
        return lax.rem(z + offset + 2 * n_z, n_z)

    sib = at(y, z, 1 - core)
    ynb = at(1 - y, z, core)
    znb = (at(y, zmod(1), core), at(y, zmod(-1), core))
    n_x = n_cores // 2
    y_hi = c // n_x
    x = lax.rem(c, n_x)
    peers = []
    for dy in range(2):
        for dx in range(n_x):
            if dy or dx:
                other = lax.rem(y_hi + dy, 2) * n_x + lax.rem(x + dx, n_x)
                peers.append((dp, other))

    sent = []

    def send(i, src, dst, dev):
        d = pltpu.make_async_remote_copy(
            src, dst, ss.at[i], rs.at[i], device_id=dev, device_id_type=MESH
        )
        d.start()
        sent.append(d)

    def arrive(i, ref):
        pltpu.make_async_remote_copy(
            ref, ref, ss.at[i], rs.at[i], device_id=sib, device_id_type=MESH
        ).wait_recv()

    loads = [
        pltpu.make_async_copy(src, dst, in_sem.at[n])
        for n, (src, dst) in enumerate(
            (
                (core_hbm, core_v),
                (og_hbm, og),
                (outf_hbm, outf),
                (tok_hbm, tok),
                (rw_hbm, rw),
                (inf_hbm, inf),
                (ef_hbm, ef),
            )
        )
    ]
    for load in loads:
        load.start()

    barrier = pltpu.get_barrier_semaphore()
    greet = [sib, ynb, znb[0], znb[1]] + peers
    for dev in greet:
        pl.semaphore_signal(barrier, inc=1, device_id=dev, device_id_type=MESH)
    loads[0].wait()
    whole[y, z, core] = jnp.swapaxes(core_v[...].astype(F32), 0, 1).astype(BF16)
    pl.semaphore_wait(barrier, len(greet))

    lane_y = (y, 1 - y)

    def ag_id(lane, way, s):
        return ids.gather_z + (lane * 2 + way) * steps + s - 1

    def ag_ref(lane, zz):
        return whole.at[lane_y[lane], zz, core]

    def ag_sib(lane, offset):
        ref = ag_ref(lane, zmod(offset))
        send(ids.gather_sib + lane * n_z + offset % n_z, ref, ref, sib)

    def ag_open(lane):
        ref = ag_ref(lane, z)
        for way in range(2):
            if hops[lane][way] >= 1:
                send(ag_id(lane, way, 1), ref, ref, znb[way])
        ag_sib(lane, 0)

    def ag_step(s, lane):
        for way in range(2):
            if s <= hops[lane][way]:
                offset = -s if way == 0 else s
                ref = ag_ref(lane, zmod(offset))
                arrive(ag_id(lane, way, s), ref)
                if s + 1 <= hops[lane][way]:
                    send(ag_id(lane, way, s + 1), ref, ref, znb[way])
                ag_sib(lane, offset)

    def ag_close():
        for lane in range(2):
            for offset in range(n_z):
                ref = whole.at[lane_y[lane], zmod(offset), 1 - core]
                arrive(ids.gather_sib + lane * n_z + offset, ref)

    behind = peers_from(y_hi, x, n_x)
    n_peers = n_cores - 1

    def sum_send(first, src, got, cols):
        for k, dev in enumerate(peers):
            send(first + k, src.at[dev[1], :, cols], got.at[k, :, cols], dev)

    def sum_wait(first, src, got, cols):
        for k in range(n_peers):
            arrive(first + k, got.at[k, :, cols])
        total = src[c, :, cols].astype(F32)
        for k in range(n_peers):
            total = total + got[k, :, cols].astype(F32)
        return total

    def share_send(first, held, cols):
        for k, dev in enumerate(peers):
            send(first + k, held.at[c, :, cols], held.at[c, :, cols], dev)

    def share_wait(first, held, cols):
        for k in range(n_peers):
            arrive(first + k, held.at[behind[k], :, cols])

    send(ids.gather_y, ag_ref(0, z), ag_ref(0, z), ynb)
    ag_open(0)

    n_go = n_g + n_o
    everything = slice(None)
    loads[1].wait()
    loads[2].wait()
    part_a[:, :, n_g:] = dot_nt(og[...], outf[...]).astype(BF16).reshape(n_cores, block, n_o)
    loads[3].wait()
    loads[4].wait()
    part_a[:, :, :n_g] = dot_nt(tok[...], rw[...]).astype(BF16).reshape(n_cores, block, n_g)
    sum_send(ids.sum_in, part_a, got_a, everything)
    loads[5].wait()
    part_p[...] = dot_nt(tok[...], inf[...]).reshape(n_cores, block, n_i)
    sum_send(ids.sum_in + n_peers, part_p, got_p, everything)
    loads[6].wait()
    ef_all[c] = ef[...].astype(F32)
    for k, dev in enumerate(peers):
        send(ids.factor + k, ef_all.at[c], ef_all.at[c], dev)

    arrive(ids.gather_y, ag_ref(1, z))
    ag_open(1)
    ag_step(1, 0)
    ag_step(1, 1)

    total = sum_wait(ids.sum_in, part_a, got_a, everything)
    gate = jax.nn.sigmoid(total[:, :n_g])
    gates[...] = gate
    held_a[c, :, :n_g] = gate.astype(BF16)
    held_a[c, :, n_g:] = total[:, n_g:].astype(BF16)
    share_send(ids.share_in, held_a, everything)

    ag_step(2, 0)

    held_p[c] = sum_wait(ids.sum_in + n_peers, part_p, got_p, everything).astype(BF16)
    share_send(ids.share_in + n_peers, held_p, everything)

    ag_step(2, 1)
    ag_step(3, 0)
    ag_step(3, 1)

    def wide(v, n):
        return jnp.concatenate([v] * (n // 128), axis=1)

    def spread_mixing(held, out):
        mixing = dot_nt(held[:, :, :n_g].reshape(rows, n_g), ef[...])
        for e in range(n_e):
            out[e] = jnp.broadcast_to(mixing[:, e : e + 1], (rows, 128))

    share_wait(ids.share_in, held_a, everything)
    send(ids.core_sib, held_a, sib_a, sib)
    spread_mixing(held_a, mix_b)
    lgrad = held_a[:, :, n_g:].reshape(rows, n_o)
    lgrad_wide = lgrad.astype(F32)

    share_wait(ids.share_in + n_peers, held_p, everything)
    proj = held_p[...].reshape(rows, n_i)
    proj_t[...] = proj.T.reshape(2 * n_z, 2, i_rows, rows)
    send(ids.core_sib + 1, proj_t.at[:, 1 - core], sib_pt, sib)
    arrive(ids.core_sib, sib_a)
    spread_mixing(sib_a, sib_mix)
    sib_lgrad = sib_a[:, :, n_g:].reshape(rows, n_o).astype(F32)
    half = 2 * n_z * i_rows
    own_t = proj_t[:, core].reshape(half, rows)
    arrive(ids.core_sib + 1, sib_pt)
    sib_t = sib_pt[...].reshape(half, rows)

    def core_terms(e, _):
        own = (wide(mix_b[e], n_o) * lgrad_wide).astype(BF16)
        other = (wide(sib_mix[e], n_o) * sib_lgrad).astype(BF16)
        term = (dot_nn(own_t, own) + dot_nn(sib_t, other)) * inv_rows
        core_b[:, :, e] = term.astype(BF16).reshape(2, n_z, i_rows, n_o)
        return 0

    lax.fori_loop(0, n_e, core_terms, 0)

    def rs_ring(block_of, sib_of, got, yr, z_id, y_id):
        def num(lane, way, s):
            return z_id + (lane * 2 + way) * steps + s - 1

        def base(lane, d):
            val = block_of(lane_y[lane], d)[...].astype(F32)
            if sib_of is not None:
                val = val + sib_of(lane_y[lane], d)[...].astype(F32)
            return val

        def step(s):
            for lane in range(2):
                for way in range(2):
                    k = hops[lane][way]
                    if s <= k:
                        far = k - s + 1
                        d = zmod(far if way == 0 else -far)
                        out = block_of(lane_y[lane], d)
                        if s > 1:
                            arrive(num(lane, way, s - 1), got.at[lane, way, s - 2])
                            val = base(lane, d) + got[lane, way, s - 2].astype(F32)
                            out[...] = val.astype(BF16)
                        elif sib_of is not None:
                            out[...] = base(lane, d).astype(BF16)
                        send(num(lane, way, s), out, got.at[lane, way, s - 1], znb[way])

        def lane_sum(lane):
            val = base(lane, z)
            for way in range(2):
                k = hops[lane][way]
                if k:
                    arrive(num(lane, way, k), got.at[lane, way, k - 1])
                    val = val + got[lane, way, k - 1].astype(F32)
            return val

        def turn():
            val = lane_sum(1)
            out = block_of(1 - y, z)
            out[...] = val.astype(BF16)
            send(y_id, out, yr, ynb)

        def end():
            val = lane_sum(0)
            arrive(y_id, yr)
            return val + yr[...].astype(F32)

        return step, turn, end

    core_step, core_turn, core_end = rs_ring(
        lambda yy, d: core_b.at[yy, d], None, core_r, core_yr, ids.core_z, ids.core_y
    )
    out_step, out_turn, out_end = rs_ring(
        lambda yy, d: fac_b.at[yy, d, core],
        lambda yy, d: fac_s.at[yy, d],
        fac_r, fac_yr, ids.out_z, ids.out_y,
    )
    inp_step, inp_turn, inp_end = rs_ring(
        lambda yy, d: inp_b.at[yy, d, core],
        lambda yy, d: inp_s.at[yy, d],
        inp_r, inp_yr, ids.inp_z, ids.inp_y,
    )

    core_step(1)
    for s in range(4, steps + 1):
        ag_step(s, 0)
        ag_step(s, 1)
    ag_close()

    lat_acc[...] = jnp.zeros_like(lat_acc)
    pg_acc[...] = jnp.zeros_like(pg_acc)
    mg_acc[...] = jnp.zeros_like(mg_acc)
    lane_no = lax.broadcasted_iota(jnp.int32, (rows, 128), 1)

    def forward(e, _):
        expanded = dot_nn(proj, whole[:, :, :, e].reshape(n_i, n_o))
        lat_acc[...] += wide(mix_b[e], n_o) * expanded
        col = jnp.sum(lgrad_wide * expanded, axis=1, keepdims=True)
        mg_acc[...] += jnp.where(lane_no == c * n_e + e, col, 0.0)
        return 0

    def backward(e, _):
        spread = dot_nt(lgrad, whole[:, :, :, e].reshape(n_i, n_o))
        pg_acc[...] += wide(mix_b[e], n_i) * spread
        return 0

    n_om = n_o + 128
    lat_mix = slice(0, n_om)
    pg_cols = slice(n_om, n_om + n_i)
    lax.fori_loop(0, n_e, forward, 0)
    part_mid[:, :, :n_o] = lat_acc[...].astype(BF16).reshape(n_cores, block, n_o)
    mix_low = mg_acc[...].astype(BF16)
    part_mid[:, :, n_o:n_om] = mix_low.reshape(n_cores, block, 128)
    sum_send(ids.sum_mid, part_mid, got_mid, lat_mix)


    lax.fori_loop(0, n_e, backward, 0)
    part_mid[:, :, pg_cols] = pg_acc[...].astype(BF16).reshape(n_cores, block, n_i)
    sum_send(ids.sum_mid + n_peers, part_mid, got_mid, pg_cols)

    gate_low = held_a[:, :, :n_g].reshape(rows, n_g)
    expert_full = dot_tn(gate_low, mix_low) * inv_rows
    pick = (
        lax.broadcasted_iota(jnp.int32, (128, 128), 0)
        == lax.broadcasted_iota(jnp.int32, (128, 128), 1) + c * n_e
    ).astype(BF16)
    expert_term = dot_nn(expert_full.astype(BF16), pick)
    core_step(2)

    for k in range(n_peers):
        arrive(ids.factor + k, ef_all.at[behind[k]])
    total = sum_wait(ids.sum_mid, part_mid, got_mid, lat_mix)
    mix_block = total[:, n_o : n_o + n_cores * n_e].astype(BF16)
    gate_grad = dot_nn(mix_block, ef_all[...].reshape(n_cores * n_e, n_g).astype(BF16))
    gate = gates[...]
    n_og = n_o + n_g
    lat_logit = slice(0, n_og)
    pg_held = slice(n_og, n_og + n_i)
    held_mid[c, :, :n_o] = total[:, :n_o].astype(BF16)
    held_mid[c, :, n_o:n_og] = (gate_grad * gate * (1.0 - gate)).astype(BF16)
    share_send(ids.share_mid, held_mid, lat_logit)

    core_step(3)

    held_mid[c, :, pg_held] = sum_wait(
        ids.sum_mid + n_peers, part_mid, got_mid, pg_cols
    ).astype(BF16)
    share_send(ids.share_mid + n_peers, held_mid, pg_held)
    for s in range(4, steps + 1):
        core_step(s)

    share_wait(ids.share_mid, held_mid, lat_logit)
    latent = held_mid[:, :, :n_o].reshape(rows, n_o)
    logit_grad = held_mid[:, :, n_o:n_og].reshape(rows, n_g)
    blk = (2, n_z, 2)
    g_rows = n_g // n_dp
    mid = width // 2
    w_router = width + mid
    fac_b[:, :, :, :, :width] = (
        (dot_tn(latent, og[...]) * inv_rows).astype(BF16).reshape(*blk, i_rows, width)
    )
    router_term = (dot_tn(logit_grad, tok[...]) * inv_rows).reshape(*blk, g_rows, width)
    fac_b[:, :, :, :, width:w_router] = jnp.concatenate(
        [router_term[..., :mid], router_term[..., mid:]], axis=3
    ).astype(BF16)
    expert_blocks = expert_term.reshape(*blk, g_rows, 128)
    fac_b[:, :, :, :, w_router:] = jnp.concatenate(
        [expert_blocks, jnp.zeros_like(expert_blocks)], axis=3
    ).astype(BF16)
    send(ids.out_sib, fac_b.at[:, :, 1 - core], fac_s, sib)


    arrive(ids.out_sib, fac_s)
    out_step(1)

    share_wait(ids.share_mid + n_peers, held_mid, pg_held)
    pgrad = held_mid[:, :, pg_held].reshape(rows, n_i)
    inp_b[...] = (dot_tn(pgrad, tok[...]) * inv_rows).astype(BF16).reshape(*blk, i_rows, width)
    send(ids.inp_sib, inp_b.at[:, :, 1 - core], inp_s, sib)

    out_step(2)
    arrive(ids.inp_sib, inp_s)
    inp_step(1)

    mixed_v[...] = dot_nn(latent, outf[...]).astype(BF16)
    results = []

    def result(src, dst):
        results.append(pltpu.make_async_copy(src, dst, out_sem.at[len(results)]))
        results[-1].start()

    result(mixed_v, mixed_ref)
    core_turn()
    out_step(3)
    inp_step(2)
    tgrad_v[...] = (dot_nn(pgrad, inf[...]) + dot_nn(logit_grad, rw[...])).astype(BF16)
    result(tgrad_v, tgrad_ref)
    for s in range(4, steps + 1):
        out_step(s)
        inp_step(s - 1)
    out_turn()
    if steps >= 4:
        inp_step(steps)
    cgrad_v[...] = jnp.swapaxes(core_end(), 0, 1)
    result(cgrad_v, cgrad_ref)
    inp_turn()
    val = out_end()
    ograd_v[...] = val[:, :width]
    rgrad_v[:, :mid] = val[:g_rows, width:w_router]
    rgrad_v[:, mid:] = val[g_rows:, width:w_router]
    egrad_v[...] = val[:g_rows, w_router : w_router + n_e]
    result(ograd_v, ograd_ref)
    result(rgrad_v, rgrad_ref)
    result(egrad_v, egrad_ref)
    igrad_v[...] = inp_end()
    result(igrad_v, igrad_ref)

    for d in sent:
        d.wait_send()
    for r in results:
        r.wait()


def hand_over(n, *refs):
    srcs, dsts, held = refs[:n], refs[n : 2 * n], refs[2 * n : 3 * n]
    in_sem, out_sem = refs[3 * n :]
    ins = [pltpu.make_async_copy(srcs[i], held[i], in_sem.at[i]) for i in range(n)]
    outs = [pltpu.make_async_copy(held[i], dsts[i], out_sem.at[i]) for i in range(n)]
    for copy in ins:
        copy.start()
    for i in range(n):
        ins[i].wait()
        outs[i].start()
    for copy in outs:
        copy.wait()


def peers_from(y_hi, x, n_x):
    out = []
    for dy in range(2):
        for dx in range(n_x):
            if dy or dx:
                out.append(lax.rem(y_hi + dy, 2) * n_x + lax.rem(x + n_x - dx, n_x))
    return out


def shards(n_dp, n_cores, tokens, router_weight, expert_factor, input_factor, core_tensor,
           output_factor, out_grad):
    n_z = n_dp // 4
    steps = n_z // 2
    rows, width = tokens.shape
    n_g = router_weight.shape[0]
    n_i = input_factor.shape[0]
    n_o = output_factor.shape[0]
    i_rows, n_e, _ = core_tensor.shape
    g_rows = n_g // n_dp
    block = rows // n_cores
    cblk = (n_e, i_rows, n_o)
    fblk = (i_rows, width + width // 2 + 128)
    iblk = (i_rows, width)
    in_cols = n_g + n_i + n_o
    mid_cols = n_o + n_i + 128
    ids = Ids(n_z, n_cores, n_e)
    sds = jax.ShapeDtypeStruct
    results = (
        sds((rows, width), BF16),
        sds((rows, width), BF16),
        sds((i_rows, n_e, n_o), F32),
        sds((i_rows, width), F32),
        sds((g_rows, width), F32),
        sds((i_rows, width), F32),
        sds((g_rows, n_e), F32),
    )
    vmem = pltpu.VMEM
    scratch = [vmem(r.shape, r.dtype) for r in results] + [
        vmem((rows, width), BF16),
        vmem((n_g, width), BF16),
        vmem((n_e, n_g), BF16),
        vmem((n_i, width), BF16),
        vmem((n_o, width), BF16),
        vmem((rows, width), BF16),
        vmem((i_rows, n_e, n_o), BF16),
        vmem((2, n_z, 2) + cblk, BF16),
        vmem((n_cores, n_e, n_g), F32),
        vmem((n_cores, block, n_g + n_o), BF16),
        vmem((n_cores - 1, block, n_g + n_o), BF16),
        vmem((n_cores, block, n_g + n_o), BF16),
        vmem((n_cores, block, n_i), F32),
        vmem((n_cores - 1, block, n_i), F32),
        vmem((n_cores, block, n_i), BF16),
        vmem((block, n_g), F32),
        vmem((n_cores, block, mid_cols), BF16),
        vmem((n_cores - 1, block, mid_cols), BF16),
        vmem((n_cores, block, in_cols), BF16),
        vmem((n_e, rows, 128), F32),
        vmem((n_cores, block, n_g + n_o), BF16),
        vmem((n_e, rows, 128), F32),
        vmem((2 * n_z, 2, i_rows, rows), BF16),
        vmem((2 * n_z, i_rows, rows), BF16),
        vmem((rows, n_o), F32),
        vmem((rows, n_i), F32),
        vmem((rows, 128), F32),
        vmem((2, n_z) + cblk, BF16),
        vmem((2, 2, steps) + cblk, BF16),
        vmem(cblk, BF16),
        vmem((2, n_z, 2) + fblk, BF16),
        vmem((2, n_z) + fblk, BF16),
        vmem((2, 2, steps) + fblk, BF16),
        vmem(fblk, BF16),
        vmem((2, n_z, 2) + iblk, BF16),
        vmem((2, n_z) + iblk, BF16),
        vmem((2, 2, steps) + iblk, BF16),
        vmem(iblk, BF16),
        pltpu.SemaphoreType.DMA((7,)),
        pltpu.SemaphoreType.DMA((7,)),
        pltpu.SemaphoreType.DMA((ids.count,)),
        pltpu.SemaphoreType.DMA((ids.count,)),
    ]
    outs = pl.pallas_call(
        functools.partial(kernel, n_z, n_cores),
        out_shape=results,
        in_specs=[pl.BlockSpec(memory_space=pl.ANY)] * 7,
        out_specs=[pl.BlockSpec(memory_space=pl.ANY)] * 7,
        scratch_shapes=scratch,
        compiler_params=pltpu.CompilerParams(
            collective_id=0, has_side_effects=True, vmem_limit_bytes=56 * 1024 * 1024
        ),
    )(tokens, router_weight, expert_factor.T, input_factor, core_tensor, output_factor, out_grad)
    return pl.pallas_call(
        functools.partial(hand_over, len(results)),
        out_shape=results,
        in_specs=[pl.BlockSpec(memory_space=pl.ANY)] * 7,
        out_specs=[pl.BlockSpec(memory_space=pl.ANY)] * 7,
        scratch_shapes=[vmem(r.shape, r.dtype) for r in results]
        + [pltpu.SemaphoreType.DMA((7,))] * 2,
    )(*outs)


def solution(mesh):
    return jax.shard_map(
        functools.partial(shards, mesh.shape["dp"], mesh.shape["cores"]),
        mesh=mesh,
        in_specs=(
            P("dp", "cores"),
            P(None, "cores"),
            P(None, "cores"),
            P(None, "cores"),
            P("dp", "cores", None),
            P(None, "cores"),
            P("dp", "cores"),
        ),
        out_specs=(
            P("dp", "cores"),
            P("dp", "cores"),
            P("dp", "cores", None),
            P("dp", "cores"),
            P("dp", "cores"),
            P("dp", "cores"),
            P("dp", "cores"),
        ),
        check_vma=False,
    )
```

```python
import functools

import jax
import jax.numpy as jnp
from jax import lax
from jax.experimental import pallas as pl
from jax.experimental.pallas import tpu as pltpu
from jax.sharding import PartitionSpec as P

MESH = pl.DeviceIdType.MESH
F32 = jnp.float32
BF16 = jnp.bfloat16


def dot_nn(a, b):
    return lax.dot_general(a, b, (((1,), (0,)), ((), ())), preferred_element_type=F32)


def dot_nt(a, b):
    return lax.dot_general(a, b, (((1,), (1,)), ((), ())), preferred_element_type=F32)


def dot_tn(a, b):
    return lax.dot_general(a, b, (((0,), (0,)), ((), ())), preferred_element_type=F32)


def ring_hops(n_z):
    up = n_z // 2
    down = n_z - 1 - up
    return ((up, down), (down, up))


class Ids:
    def __init__(self, n_z, n_cores, n_e):
        self.count = 0
        steps = n_z // 2
        self.gather_y = self.take(1)
        self.gather_z = self.take(4 * steps)
        self.gather_sib = self.take(2 * n_z)
        self.factor = self.take(n_cores - 1)
        self.sum_in = self.take(2 * (n_cores - 1))
        self.share_in = self.take(2 * (n_cores - 1))
        self.sum_mid = self.take(2 * (n_cores - 1))
        self.share_mid = self.take(2 * (n_cores - 1))
        self.core_sib = self.take(2)
        self.core_z = self.take(4 * steps)
        self.core_y = self.take(1)
        self.out_sib = self.take(1)
        self.out_z = self.take(4 * steps)
        self.out_y = self.take(1)
        self.inp_sib = self.take(1)
        self.inp_z = self.take(4 * steps)
        self.inp_y = self.take(1)

    def take(self, n):
        first = self.count
        self.count += n
        return first


def kernel(
    n_z, n_cores,
    tok_hbm, rw_hbm, ef_hbm, inf_hbm, core_hbm, outf_hbm, og_hbm,
    mixed_ref, tgrad_ref, cgrad_ref, igrad_ref, rgrad_ref, ograd_ref, egrad_ref,
    mixed_v, tgrad_v, cgrad_v, igrad_v, rgrad_v, ograd_v, egrad_v,
    tok, rw, ef, inf, outf, og, core_v,
    whole, ef_all, part_a, got_a, held_a, part_p, got_p, held_p, gates, part_mid, got_mid, held_mid,
    mix_b, sib_a, sib_mix, proj_t, sib_pt, lat_acc, pg_acc, mg_acc,
    core_b, core_r, core_yr,
    fac_b, fac_s, fac_r, fac_yr,
    inp_b, inp_s, inp_r, inp_yr,
    in_sem, out_sem, ss, rs,
):
    rows, width = tok.shape
    n_g = rw.shape[0]
    n_i = inf.shape[0]
    n_o = outf.shape[0]
    n_e = ef.shape[0]
    block = rows // n_cores
    i_rows = whole.shape[4]
    n_dp = 4 * n_z
    inv_rows = 1.0 / rows
    ids = Ids(n_z, n_cores, n_e)
    steps = n_z // 2
    hops = ring_hops(n_z)

    dp = lax.axis_index("dp")
    c = lax.axis_index("cores")
    core = lax.rem(dp, 2)
    z = lax.rem(dp // 2, n_z)
    y = dp // (2 * n_z)

    def at(yy, zz, kk):
        return ((yy * n_z + zz) * 2 + kk, c)

    def zmod(offset):
        return lax.rem(z + offset + 2 * n_z, n_z)

    sib = at(y, z, 1 - core)
    ynb = at(1 - y, z, core)
    znb = (at(y, zmod(1), core), at(y, zmod(-1), core))
    n_x = n_cores // 2
    y_hi = c // n_x
    x = lax.rem(c, n_x)
    peers = []
    for dy in range(2):
        for dx in range(n_x):
            if dy or dx:
                other = lax.rem(y_hi + dy, 2) * n_x + lax.rem(x + dx, n_x)
                peers.append((dp, other))

    sent = []

    def send(i, src, dst, dev):
        d = pltpu.make_async_remote_copy(
            src, dst, ss.at[i], rs.at[i], device_id=dev, device_id_type=MESH
        )
        d.start()
        sent.append(d)

    def arrive(i, ref):
        pltpu.make_async_remote_copy(
            ref, ref, ss.at[i], rs.at[i], device_id=sib, device_id_type=MESH
        ).wait_recv()

    loads = [
        pltpu.make_async_copy(src, dst, in_sem.at[n])
        for n, (src, dst) in enumerate(
            (
                (core_hbm, core_v),
                (og_hbm, og),
                (outf_hbm, outf),
                (tok_hbm, tok),
                (rw_hbm, rw),
                (inf_hbm, inf),
                (ef_hbm, ef),
            )
        )
    ]
    for load in loads:
        load.start()

    barrier = pltpu.get_barrier_semaphore()
    greet = [sib, ynb, znb[0], znb[1]] + peers
    for dev in greet:
        pl.semaphore_signal(barrier, inc=1, device_id=dev, device_id_type=MESH)
    loads[0].wait()
    whole[y, z, core] = jnp.swapaxes(core_v[...].astype(F32), 0, 1).astype(BF16)
    pl.semaphore_wait(barrier, len(greet))

    lane_y = (y, 1 - y)

    def ag_id(lane, way, s):
        return ids.gather_z + (lane * 2 + way) * steps + s - 1

    def ag_ref(lane, zz):
        return whole.at[lane_y[lane], zz, core]

    def ag_sib(lane, offset):
        ref = ag_ref(lane, zmod(offset))
        send(ids.gather_sib + lane * n_z + offset % n_z, ref, ref, sib)

    def ag_open(lane):
        ref = ag_ref(lane, z)
        for way in range(2):
            if hops[lane][way] >= 1:
                send(ag_id(lane, way, 1), ref, ref, znb[way])
        ag_sib(lane, 0)

    def ag_step(s, lane):
        for way in range(2):
            if s <= hops[lane][way]:
                offset = -s if way == 0 else s
                ref = ag_ref(lane, zmod(offset))
                arrive(ag_id(lane, way, s), ref)
                if s + 1 <= hops[lane][way]:
                    send(ag_id(lane, way, s + 1), ref, ref, znb[way])
                ag_sib(lane, offset)

    def ag_close():
        for lane in range(2):
            for offset in range(n_z):
                ref = whole.at[lane_y[lane], zmod(offset), 1 - core]
                arrive(ids.gather_sib + lane * n_z + offset, ref)

    behind = peers_from(y_hi, x, n_x)
    n_peers = n_cores - 1

    def sum_send(first, src, got, cols):
        for k, dev in enumerate(peers):
            send(first + k, src.at[dev[1], :, cols], got.at[k, :, cols], dev)

    def sum_wait(first, src, got, cols):
        for k in range(n_peers):
            arrive(first + k, got.at[k, :, cols])
        total = src[c, :, cols].astype(F32)
        for k in range(n_peers):
            total = total + got[k, :, cols].astype(F32)
        return total

    def share_send(first, held, cols):
        for k, dev in enumerate(peers):
            send(first + k, held.at[c, :, cols], held.at[c, :, cols], dev)

    def share_wait(first, held, cols):
        for k in range(n_peers):
            arrive(first + k, held.at[behind[k], :, cols])

    send(ids.gather_y, ag_ref(0, z), ag_ref(0, z), ynb)
    ag_open(0)

    n_go = n_g + n_o
    everything = slice(None)
    loads[1].wait()
    loads[2].wait()
    part_a[:, :, n_g:] = dot_nt(og[...], outf[...]).astype(BF16).reshape(n_cores, block, n_o)
    loads[3].wait()
    loads[4].wait()
    part_a[:, :, :n_g] = dot_nt(tok[...], rw[...]).astype(BF16).reshape(n_cores, block, n_g)
    sum_send(ids.sum_in, part_a, got_a, everything)
    loads[5].wait()
    part_p[...] = dot_nt(tok[...], inf[...]).reshape(n_cores, block, n_i)
    sum_send(ids.sum_in + n_peers, part_p, got_p, everything)
    loads[6].wait()
    ef_all[c] = ef[...].astype(F32)
    for k, dev in enumerate(peers):
        send(ids.factor + k, ef_all.at[c], ef_all.at[c], dev)

    arrive(ids.gather_y, ag_ref(1, z))
    ag_open(1)
    ag_step(1, 0)
    ag_step(1, 1)

    total = sum_wait(ids.sum_in, part_a, got_a, everything)
    gate = jax.nn.sigmoid(total[:, :n_g])
    gates[...] = gate
    held_a[c, :, :n_g] = gate.astype(BF16)
    held_a[c, :, n_g:] = total[:, n_g:].astype(BF16)
    share_send(ids.share_in, held_a, everything)

    ag_step(2, 0)

    held_p[c] = sum_wait(ids.sum_in + n_peers, part_p, got_p, everything).astype(BF16)
    share_send(ids.share_in + n_peers, held_p, everything)

    ag_step(2, 1)
    ag_step(3, 0)
    ag_step(3, 1)

    def wide(v, n):
        return jnp.concatenate([v] * (n // 128), axis=1)

    def spread_mixing(held, out):
        mixing = dot_nt(held[:, :, :n_g].reshape(rows, n_g), ef[...])
        for e in range(n_e):
            out[e] = jnp.broadcast_to(mixing[:, e : e + 1], (rows, 128))

    share_wait(ids.share_in, held_a, everything)
    send(ids.core_sib, held_a, sib_a, sib)
    spread_mixing(held_a, mix_b)
    lgrad = held_a[:, :, n_g:].reshape(rows, n_o)
    lgrad_wide = lgrad.astype(F32)

    share_wait(ids.share_in + n_peers, held_p, everything)
    proj = held_p[...].reshape(rows, n_i)
    proj_t[...] = proj.T.reshape(2 * n_z, 2, i_rows, rows)
    send(ids.core_sib + 1, proj_t.at[:, 1 - core], sib_pt, sib)
    arrive(ids.core_sib, sib_a)
    spread_mixing(sib_a, sib_mix)
    sib_lgrad = sib_a[:, :, n_g:].reshape(rows, n_o).astype(F32)
    half = 2 * n_z * i_rows
    own_t = proj_t[:, core].reshape(half, rows)
    arrive(ids.core_sib + 1, sib_pt)
    sib_t = sib_pt[...].reshape(half, rows)

    def core_terms(e, _):
        own = (wide(mix_b[e], n_o) * lgrad_wide).astype(BF16)
        other = (wide(sib_mix[e], n_o) * sib_lgrad).astype(BF16)
        term = (dot_nn(own_t, own) + dot_nn(sib_t, other)) * inv_rows
        core_b[:, :, e] = term.astype(BF16).reshape(2, n_z, i_rows, n_o)
        return 0

    lax.fori_loop(0, n_e, core_terms, 0)

    def rs_ring(block_of, sib_of, got, yr, z_id, y_id):
        def num(lane, way, s):
            return z_id + (lane * 2 + way) * steps + s - 1

        def base(lane, d):
            val = block_of(lane_y[lane], d)[...].astype(F32)
            if sib_of is not None:
                val = val + sib_of(lane_y[lane], d)[...].astype(F32)
            return val

        def step(s):
            for lane in range(2):
                for way in range(2):
                    k = hops[lane][way]
                    if s <= k:
                        far = k - s + 1
                        d = zmod(far if way == 0 else -far)
                        out = block_of(lane_y[lane], d)
                        if s > 1:
                            arrive(num(lane, way, s - 1), got.at[lane, way, s - 2])
                            val = base(lane, d) + got[lane, way, s - 2].astype(F32)
                            out[...] = val.astype(BF16)
                        elif sib_of is not None:
                            out[...] = base(lane, d).astype(BF16)
                        send(num(lane, way, s), out, got.at[lane, way, s - 1], znb[way])

        def lane_sum(lane):
            val = base(lane, z)
            for way in range(2):
                k = hops[lane][way]
                if k:
                    arrive(num(lane, way, k), got.at[lane, way, k - 1])
                    val = val + got[lane, way, k - 1].astype(F32)
            return val

        def turn():
            val = lane_sum(1)
            out = block_of(1 - y, z)
            out[...] = val.astype(BF16)
            send(y_id, out, yr, ynb)

        def end():
            val = lane_sum(0)
            arrive(y_id, yr)
            return val + yr[...].astype(F32)

        return step, turn, end

    core_step, core_turn, core_end = rs_ring(
        lambda yy, d: core_b.at[yy, d], None, core_r, core_yr, ids.core_z, ids.core_y
    )
    out_step, out_turn, out_end = rs_ring(
        lambda yy, d: fac_b.at[yy, d, core],
        lambda yy, d: fac_s.at[yy, d],
        fac_r, fac_yr, ids.out_z, ids.out_y,
    )
    inp_step, inp_turn, inp_end = rs_ring(
        lambda yy, d: inp_b.at[yy, d, core],
        lambda yy, d: inp_s.at[yy, d],
        inp_r, inp_yr, ids.inp_z, ids.inp_y,
    )

    core_step(1)
    for s in range(4, steps + 1):
        ag_step(s, 0)
        ag_step(s, 1)
    ag_close()

    lat_acc[...] = jnp.zeros_like(lat_acc)
    pg_acc[...] = jnp.zeros_like(pg_acc)
    mg_acc[...] = jnp.zeros_like(mg_acc)
    lane_no = lax.broadcasted_iota(jnp.int32, (rows, 128), 1)

    def forward(e, _):
        expanded = dot_nn(proj, whole[:, :, :, e].reshape(n_i, n_o))
        lat_acc[...] += wide(mix_b[e], n_o) * expanded
        col = jnp.sum(lgrad_wide * expanded, axis=1, keepdims=True)
        mg_acc[...] += jnp.where(lane_no == c * n_e + e, col, 0.0)
        return 0

    def backward(e, _):
        spread = dot_nt(lgrad, whole[:, :, :, e].reshape(n_i, n_o))
        pg_acc[...] += wide(mix_b[e], n_i) * spread
        return 0

    n_om = n_o + 128
    lat_mix = slice(0, n_om)
    pg_cols = slice(n_om, n_om + n_i)
    lax.fori_loop(0, n_e, forward, 0)
    part_mid[:, :, :n_o] = lat_acc[...].astype(BF16).reshape(n_cores, block, n_o)
    mix_low = mg_acc[...].astype(BF16)
    part_mid[:, :, n_o:n_om] = mix_low.reshape(n_cores, block, 128)
    sum_send(ids.sum_mid, part_mid, got_mid, lat_mix)


    lax.fori_loop(0, n_e, backward, 0)
    part_mid[:, :, pg_cols] = pg_acc[...].astype(BF16).reshape(n_cores, block, n_i)
    sum_send(ids.sum_mid + n_peers, part_mid, got_mid, pg_cols)

    gate_low = held_a[:, :, :n_g].reshape(rows, n_g)
    expert_full = dot_tn(gate_low, mix_low) * inv_rows
    pick = (
        lax.broadcasted_iota(jnp.int32, (128, 128), 0)
        == lax.broadcasted_iota(jnp.int32, (128, 128), 1) + c * n_e
    ).astype(BF16)
    expert_term = dot_nn(expert_full.astype(BF16), pick)
    core_step(2)

    for k in range(n_peers):
        arrive(ids.factor + k, ef_all.at[behind[k]])
    total = sum_wait(ids.sum_mid, part_mid, got_mid, lat_mix)
    mix_block = total[:, n_o : n_o + n_cores * n_e].astype(BF16)
    gate_grad = dot_nn(mix_block, ef_all[...].reshape(n_cores * n_e, n_g).astype(BF16))
    gate = gates[...]
    n_og = n_o + n_g
    lat_logit = slice(0, n_og)
    pg_held = slice(n_og, n_og + n_i)
    held_mid[c, :, :n_o] = total[:, :n_o].astype(BF16)
    held_mid[c, :, n_o:n_og] = (gate_grad * gate * (1.0 - gate)).astype(BF16)
    share_send(ids.share_mid, held_mid, lat_logit)

    core_step(3)

    held_mid[c, :, pg_held] = sum_wait(
        ids.sum_mid + n_peers, part_mid, got_mid, pg_cols
    ).astype(BF16)
    share_send(ids.share_mid + n_peers, held_mid, pg_held)
    for s in range(4, steps + 1):
        core_step(s)

    share_wait(ids.share_mid, held_mid, lat_logit)
    latent = held_mid[:, :, :n_o].reshape(rows, n_o)
    logit_grad = held_mid[:, :, n_o:n_og].reshape(rows, n_g)
    blk = (2, n_z, 2)
    g_rows = n_g // n_dp
    mid = width // 2
    w_router = width + mid
    fac_b[:, :, :, :, :width] = (
        (dot_tn(latent, og[...]) * inv_rows).astype(BF16).reshape(*blk, i_rows, width)
    )
    router_term = (dot_tn(logit_grad, tok[...]) * inv_rows).reshape(*blk, g_rows, width)
    fac_b[:, :, :, :, width:w_router] = jnp.concatenate(
        [router_term[..., :mid], router_term[..., mid:]], axis=3
    ).astype(BF16)
    expert_blocks = expert_term.reshape(*blk, g_rows, 128)
    fac_b[:, :, :, :, w_router:] = jnp.concatenate(
        [expert_blocks, jnp.zeros_like(expert_blocks)], axis=3
    ).astype(BF16)
    send(ids.out_sib, fac_b.at[:, :, 1 - core], fac_s, sib)


    mixed_v[...] = dot_nn(latent, outf[...]).astype(BF16)
    results = []

    def result(src, dst):
        results.append(pltpu.make_async_copy(src, dst, out_sem.at[len(results)]))
        results[-1].start()

    result(mixed_v, mixed_ref)
    arrive(ids.out_sib, fac_s)
    out_step(1)

    share_wait(ids.share_mid + n_peers, held_mid, pg_held)
    pgrad = held_mid[:, :, pg_held].reshape(rows, n_i)
    inp_b[...] = (dot_tn(pgrad, tok[...]) * inv_rows).astype(BF16).reshape(*blk, i_rows, width)
    send(ids.inp_sib, inp_b.at[:, :, 1 - core], inp_s, sib)

    out_step(2)
    tgrad_v[...] = (dot_nn(pgrad, inf[...]) + dot_nn(logit_grad, rw[...])).astype(BF16)
    result(tgrad_v, tgrad_ref)
    arrive(ids.inp_sib, inp_s)
    inp_step(1)

    core_turn()
    out_step(3)
    inp_step(2)
    for s in range(4, steps + 1):
        out_step(s)
        inp_step(s - 1)
    out_turn()
    if steps >= 4:
        inp_step(steps)
    cgrad_v[...] = jnp.swapaxes(core_end(), 0, 1)
    result(cgrad_v, cgrad_ref)
    inp_turn()
    val = out_end()
    ograd_v[...] = val[:, :width]
    rgrad_v[:, :mid] = val[:g_rows, width:w_router]
    rgrad_v[:, mid:] = val[g_rows:, width:w_router]
    egrad_v[...] = val[:g_rows, w_router : w_router + n_e]
    result(ograd_v, ograd_ref)
    result(rgrad_v, rgrad_ref)
    result(egrad_v, egrad_ref)
    igrad_v[...] = inp_end()
    result(igrad_v, igrad_ref)

    for d in sent:
        d.wait_send()
    for r in results:
        r.wait()


def hand_over(n, *refs):
    srcs, dsts, held = refs[:n], refs[n : 2 * n], refs[2 * n : 3 * n]
    in_sem, out_sem = refs[3 * n :]
    ins = [pltpu.make_async_copy(srcs[i], held[i], in_sem.at[i]) for i in range(n)]
    outs = [pltpu.make_async_copy(held[i], dsts[i], out_sem.at[i]) for i in range(n)]
    for copy in ins:
        copy.start()
    for i in range(n):
        ins[i].wait()
        outs[i].start()
    for copy in outs:
        copy.wait()


def peers_from(y_hi, x, n_x):
    out = []
    for dy in range(2):
        for dx in range(n_x):
            if dy or dx:
                out.append(lax.rem(y_hi + dy, 2) * n_x + lax.rem(x + n_x - dx, n_x))
    return out


def shards(n_dp, n_cores, tokens, router_weight, expert_factor, input_factor, core_tensor,
           output_factor, out_grad):
    n_z = n_dp // 4
    steps = n_z // 2
    rows, width = tokens.shape
    n_g = router_weight.shape[0]
    n_i = input_factor.shape[0]
    n_o = output_factor.shape[0]
    i_rows, n_e, _ = core_tensor.shape
    g_rows = n_g // n_dp
    block = rows // n_cores
    cblk = (n_e, i_rows, n_o)
    fblk = (i_rows, width + width // 2 + 128)
    iblk = (i_rows, width)
    in_cols = n_g + n_i + n_o
    mid_cols = n_o + n_i + 128
    ids = Ids(n_z, n_cores, n_e)
    sds = jax.ShapeDtypeStruct
    results = (
        sds((rows, width), BF16),
        sds((rows, width), BF16),
        sds((i_rows, n_e, n_o), F32),
        sds((i_rows, width), F32),
        sds((g_rows, width), F32),
        sds((i_rows, width), F32),
        sds((g_rows, n_e), F32),
    )
    vmem = pltpu.VMEM
    scratch = [vmem(r.shape, r.dtype) for r in results] + [
        vmem((rows, width), BF16),
        vmem((n_g, width), BF16),
        vmem((n_e, n_g), BF16),
        vmem((n_i, width), BF16),
        vmem((n_o, width), BF16),
        vmem((rows, width), BF16),
        vmem((i_rows, n_e, n_o), BF16),
        vmem((2, n_z, 2) + cblk, BF16),
        vmem((n_cores, n_e, n_g), F32),
        vmem((n_cores, block, n_g + n_o), BF16),
        vmem((n_cores - 1, block, n_g + n_o), BF16),
        vmem((n_cores, block, n_g + n_o), BF16),
        vmem((n_cores, block, n_i), F32),
        vmem((n_cores - 1, block, n_i), F32),
        vmem((n_cores, block, n_i), BF16),
        vmem((block, n_g), F32),
        vmem((n_cores, block, mid_cols), BF16),
        vmem((n_cores - 1, block, mid_cols), BF16),
        vmem((n_cores, block, in_cols), BF16),
        vmem((n_e, rows, 128), F32),
        vmem((n_cores, block, n_g + n_o), BF16),
        vmem((n_e, rows, 128), F32),
        vmem((2 * n_z, 2, i_rows, rows), BF16),
        vmem((2 * n_z, i_rows, rows), BF16),
        vmem((rows, n_o), F32),
        vmem((rows, n_i), F32),
        vmem((rows, 128), F32),
        vmem((2, n_z) + cblk, BF16),
        vmem((2, 2, steps) + cblk, BF16),
        vmem(cblk, BF16),
        vmem((2, n_z, 2) + fblk, BF16),
        vmem((2, n_z) + fblk, BF16),
        vmem((2, 2, steps) + fblk, BF16),
        vmem(fblk, BF16),
        vmem((2, n_z, 2) + iblk, BF16),
        vmem((2, n_z) + iblk, BF16),
        vmem((2, 2, steps) + iblk, BF16),
        vmem(iblk, BF16),
        pltpu.SemaphoreType.DMA((7,)),
        pltpu.SemaphoreType.DMA((7,)),
        pltpu.SemaphoreType.DMA((ids.count,)),
        pltpu.SemaphoreType.DMA((ids.count,)),
    ]
    outs = pl.pallas_call(
        functools.partial(kernel, n_z, n_cores),
        out_shape=results,
        in_specs=[pl.BlockSpec(memory_space=pl.ANY)] * 7,
        out_specs=[pl.BlockSpec(memory_space=pl.ANY)] * 7,
        scratch_shapes=scratch,
        compiler_params=pltpu.CompilerParams(
            collective_id=0, has_side_effects=True, vmem_limit_bytes=56 * 1024 * 1024
        ),
    )(tokens, router_weight, expert_factor.T, input_factor, core_tensor, output_factor, out_grad)
    return pl.pallas_call(
        functools.partial(hand_over, len(results)),
        out_shape=results,
        in_specs=[pl.BlockSpec(memory_space=pl.ANY)] * 7,
        out_specs=[pl.BlockSpec(memory_space=pl.ANY)] * 7,
        scratch_shapes=[vmem(r.shape, r.dtype) for r in results]
        + [pltpu.SemaphoreType.DMA((7,))] * 2,
    )(*outs)


def solution(mesh):
    return jax.shard_map(
        functools.partial(shards, mesh.shape["dp"], mesh.shape["cores"]),
        mesh=mesh,
        in_specs=(
            P("dp", "cores"),
            P(None, "cores"),
            P(None, "cores"),
            P(None, "cores"),
            P("dp", "cores", None),
            P(None, "cores"),
            P("dp", "cores"),
        ),
        out_specs=(
            P("dp", "cores"),
            P("dp", "cores"),
            P("dp", "cores", None),
            P("dp", "cores"),
            P("dp", "cores"),
            P("dp", "cores"),
            P("dp", "cores"),
        ),
        check_vma=False,
    )
```
